32 devices in a mesh: dp: 2 (over core), ctx: 4 (over y, x), tensor: 4 (over z).
Axes of the slice: x: 2, y: 2, z: 4, core: 2. Of those that a mesh axis runs over, the one named last changes fastest.
Arguments:
- tokens: bfloat16 [8192, 768], P(('dp', 'ctx')), may hold values from -6 to 6
- segments: int32 [8192], P(('dp', 'ctx')), may hold values from 0 to 2, as said below
- in_gain: float32 [2, 768], replicated, may hold values from 0.5 to 1.5
- gate_weight: bfloat16 [2, 768, 1536], P(None, None, 'tensor'), may hold values from -0.21875 to 0.21875
- value_weight: bfloat16 [2, 768, 1536], P(None, None, 'tensor'), may hold values from -0.21875 to 0.21875
- state_weight: bfloat16 [2, 768, 256], replicated, may hold values from -0.21875 to 0.21875
- step_weight: bfloat16 [2, 768, 24], P(None, None, 'tensor'), may hold values from -0.21875 to 0.21875
- value_filter: float32 [2, 4, 1536], P(None, None, 'tensor'), may hold values from -3 to 3
- value_offset: float32 [2, 1536], P(None, 'tensor'), may hold values from -1.5 to 1.5
- state_filter: float32 [2, 4, 256], replicated, may hold values from -3 to 3
- state_offset: float32 [2, 256], replicated, may hold values from -1.5 to 1.5
- step_bias: float32 [2, 24], P(None, 'tensor'), may hold values from -11 to -1
- decay_log: float32 [2, 24], P(None, 'tensor'), may hold values from 0 to 1.5
- skip_gain: float32 [2, 24], P(None, 'tensor'), may hold values from 0.5 to 1.5
- out_gain: float32 [2, 1536], P(None, 'tensor'), may hold values from 0.5 to 1.5
- out_weight: bfloat16 [2, 1536, 768], P(None, 'tensor'), may hold values from -0.15625 to 0.15625
- cotangent: bfloat16 [8192, 768], P(('dp', 'ctx')), may hold values from -6 to 6
Outputs:
- mixed: bfloat16 [8192, 768], P(('dp', 'ctx'))
- input_grad: bfloat16 [8192, 768], P(('dp', 'ctx'))
- grad_in_gain: float32 [2, 768], replicated
- grad_gate_weight: float32 [2, 768, 1536], P(None, None, 'tensor')
- grad_value_weight: float32 [2, 768, 1536], P(None, None, 'tensor')
- grad_state_weight: float32 [2, 768, 256], replicated
- grad_step_weight: float32 [2, 768, 24], P(None, None, 'tensor')
- grad_value_filter: float32 [2, 4, 1536], P(None, None, 'tensor')
- grad_value_offset: float32 [2, 1536], P(None, 'tensor')
- grad_state_filter: float32 [2, 4, 256], replicated
- grad_state_offset: float32 [2, 256], replicated
- grad_step_bias: float32 [2, 24], P(None, 'tensor')
- grad_decay_log: float32 [2, 24], P(None, 'tensor')
- grad_skip_gain: float32 [2, 24], P(None, 'tensor')
- grad_out_gain: float32 [2, 1536], P(None, 'tensor')
- grad_out_weight: float32 [2, 1536, 768], P(None, 'tensor')
The draws below stay inside these ranges and needn't reach their ends.
Inputs may be any that keep to these rules, and one draw needn't show every extreme that they name: `segments`: along each sequence of 4096 tokens the numbers start at 0 and rise by 0 or 1 from one token to the next. Each sequence holds three documents: the first ends inside its first piece of 1024 tokens, the last begins inside its last piece, so the middle one reaches from the first piece to the last.
All inputs are finite; a program needn't handle non-finite values.
Results may differ from the reference program's by a relative error of at most 0.028.
Values sent between devices are 32-bit elements; how exact they have to be, the bound alone decides.
No kernel may reach another device: no remote copies, remote signals or barrier semaphores. Data moves between devices by JAX's collectives and lax.ppermute only.
A program may use at most 192 MiB of HBM per device.

```python
import jax
import jax.numpy as jnp
from jax import lax

D = 768
HEADS = 24
HEADDIM = 64
STATE = 128
CONV = 4
GROUP = 256
LAYERS = 2
TOK_DEV = 1024
INNER = 1536
SEQ_LEN = 4096
SEQS = 2
TOKENS = 8192


def draw_segments(key, part):
    key = jax.random.fold_in(key, 11)
    key_flip, key_near_a, key_far_a, key_near_b, key_far_b = jax.random.split(key, 5)
    far_reach = max(CONV, TOK_DEV * 3 // 5)
    flip = jax.random.randint(key_flip, (1,), 0, 2)
    order = jnp.arange(SEQS)
    near_first = (order + flip) % 2 == 0
    first_near = jax.random.randint(key_near_a, (SEQS,), 1, CONV)
    first_far = jax.random.randint(key_far_a, (SEQS,), CONV, far_reach + 1)
    last_near = jax.random.randint(key_near_b, (SEQS,), 1, CONV)
    last_far = jax.random.randint(key_far_b, (SEQS,), CONV, far_reach + 1)
    first_back = jnp.where(near_first, first_near, first_far)
    last_into = jnp.where(near_first, last_far, last_near)
    head_pos = (TOK_DEV - first_back)[:, None]
    foot_pos = (SEQ_LEN - TOK_DEV + last_into)[:, None]
    places = jnp.arange(SEQ_LEN)[None, :]
    numbers = (places >= head_pos).astype(jnp.int32) + (places >= foot_pos).astype(jnp.int32)
    return numbers.reshape(TOKENS).astype(jnp.int32)


def draw_step_bias(key, part):
    key = jax.random.fold_in(key, 23)
    key_pick, key_slow, key_fast = jax.random.split(key, 3)
    share = 0.5
    slower = jax.random.uniform(key_pick, (LAYERS, HEADS)) < share
    slow_vals = jax.random.uniform(key_slow, (LAYERS, HEADS), minval=-11.0, maxval=-9.0)
    fast_vals = jax.random.uniform(key_fast, (LAYERS, HEADS), minval=-3.0, maxval=-1.0)
    return jnp.where(slower, slow_vals, fast_vals).astype(jnp.float32)


def block_scale(stream_key, shape, shards, least, top_value):
    loudness, own = 1.0, jax.random.fold_in(stream_key, 6)
    for dim, shards_of in shards:
        heights = jnp.exp(jax.random.uniform(jax.random.fold_in(own, dim), (shards_of,), jnp.float32, least / len(shards), top_value / len(shards)))
        loudness = loudness * jnp.repeat(heights, shape[dim] // shards_of).reshape([-1 if axis == dim else 1 for axis in range(len(shape))])
    return loudness


def noise(key, shape, scale, bound, cuts=(), held_as=jnp.bfloat16):
    level = block_scale(key, shape, cuts, -0.22, 0.18) if cuts else 1.0
    values = jax.random.normal(key, shape, jnp.float32) * scale * level
    return jnp.minimum(jnp.maximum(values, -bound), bound).astype(held_as)


def setup_inputs(seed: int = 0) -> dict:
    key_of = jax.random.split(jax.random.key(seed), 18)
    return {
        "tokens": noise(key_of[0], (TOKENS, D), 1.0, 6.0, ((0, 8),)),
        "segments": draw_segments(jax.random.fold_in(key_of[17], 71), 0),
        "in_gain": jnp.clip(1.0 + 0.1 * jax.random.normal(key_of[2], (LAYERS, D), jnp.float32), 0.5, 1.5),
        "gate_weight": noise(key_of[3], (LAYERS, D, INNER), D ** -0.5, 0.21875, ((2, 4),)),
        "value_weight": noise(key_of[4], (LAYERS, D, INNER), D ** -0.5, 0.21875, ((2, 4),)),
        "state_weight": noise(key_of[5], (LAYERS, D, 2 * STATE), D ** -0.5, 0.21875),
        "step_weight": noise(key_of[6], (LAYERS, D, HEADS), D ** -0.5, 0.21875, ((2, 4),)),
        "value_filter": noise(key_of[7], (LAYERS, CONV, INNER), CONV ** -0.5, 3.0, ((2, 4),), jnp.float32),
        "value_offset": noise(key_of[8], (LAYERS, INNER), 0.3, 1.5, ((1, 4),), jnp.float32),
        "state_filter": noise(key_of[9], (LAYERS, CONV, 2 * STATE), CONV ** -0.5, 3.0, (), jnp.float32),
        "state_offset": noise(key_of[10], (LAYERS, 2 * STATE), 0.3, 1.5, (), jnp.float32),
        "step_bias": draw_step_bias(jax.random.fold_in(key_of[17], 71), 0),
        "decay_log": jnp.clip(1.5 * jax.random.uniform(key_of[12], (LAYERS, HEADS), jnp.float32) ** block_scale(key_of[12], (LAYERS, HEADS), ((1, 4),), -0.2, 0.2), 0.0, 1.5),
        "skip_gain": jnp.clip(0.5 + 1.0 * jax.random.uniform(key_of[13], (LAYERS, HEADS), jnp.float32) ** block_scale(key_of[13], (LAYERS, HEADS), ((1, 4),), -0.2, 0.2), 0.5, 1.5),
        "out_gain": jnp.clip(1.0 + 0.1 * jax.random.normal(key_of[14], (LAYERS, INNER), jnp.float32), 0.5, 1.5),
        "out_weight": noise(key_of[15], (LAYERS, INNER, D), INNER ** -0.5, 0.15625, ((1, 4),)),
        "cotangent": noise(key_of[16], (TOKENS, D), 1.0, 6.0, ((0, 8),)),
    }


EPSILON = 1e-05
PRECISE = lax.Precision.HIGHEST

@jax.custom_vjp
def low(v):
    return lax.optimization_barrier(v.astype(jnp.bfloat16)).astype(jnp.float32)

@jax.custom_vjp
def low_back(v):
    return v

def low_keep(v):
    return (low(v), None)

def low_pass(kept, grad):
    return (grad,)

def back_keep(v):
    return (v, None)

def back_low(kept, grad):
    return (low(grad),)
low.defvjp(low_keep, low_pass)
low_back.defvjp(back_keep, back_low)

def matmul(left, right):
    return jnp.einsum('sti,ij->stj', left, right, precision=PRECISE)

def ssd_block(carry, inputs):
    state, seg_prev = carry
    head_vals, steps, log_decay, write_vec, read_vec, seg = inputs
    cumlog = jnp.cumsum(log_decay, axis=1)
    span = seg.shape[1]
    place = jnp.arange(span)
    lower = place[:, None] >= place[None, :]
    within = (lower[None] & (seg[:, :, None] == seg[:, None, :]))[..., None]
    gap = cumlog[:, :, None, :] - cumlog[:, None, :, :]
    decay = jnp.where(within, jnp.exp(jnp.where(within, gap, 0.0)), 0.0)
    intersection = jnp.einsum('sin,sjn->sij', read_vec, write_vec, precision=PRECISE)
    mixing = intersection[..., None] * decay * steps[:, None, :, :]
    output = jnp.einsum('sijh,sjhp->sihp', mixing, head_vals, precision=PRECISE)
    enter = jnp.where((seg == seg_prev[:, None])[..., None], jnp.exp(cumlog), 0.0)
    output = output + jnp.einsum('sin,shpn->sihp', read_vec, state, precision=PRECISE) * enter[..., None]
    final_seg = seg[:, -1]
    tail = jnp.where((seg == final_seg[:, None])[..., None], jnp.exp(cumlog[:, -1:, :] - cumlog), 0.0)
    retain = jnp.where((final_seg == seg_prev)[:, None], jnp.exp(cumlog[:, -1, :]), 0.0)
    state = retain[:, :, None, None] * state + jnp.einsum('sjh,sjhp,sjn->shpn', tail * steps, head_vals, write_vec, precision=PRECISE)
    return ((state, final_seg), output)

def ssd(head_vals, write_vec, read_vec, steps, log_decay, seg):
    seqs, length = seg.shape
    blocks = length // GROUP

    def split_blocks(array):
        return jnp.swapaxes(array.reshape((seqs, blocks, GROUP) + array.shape[2:]), 0, 1)
    start = (jnp.zeros((seqs, HEADS, HEADDIM, STATE), head_vals.dtype), seg[:, 0])
    _, outputs = lax.scan(jax.checkpoint(ssd_block), start, (split_blocks(head_vals), split_blocks(steps), split_blocks(log_decay), split_blocks(write_vec), split_blocks(read_vec), split_blocks(seg)))
    return jnp.swapaxes(outputs, 0, 1).reshape(seqs, length, HEADS, HEADDIM)

def layer_forward(resid, seg, weights):
    gain_in, gate_w, value_w, state_w, step_w, value_filt, value_off, state_filt, state_off, bias_step, decay_param, skip_param, gain_out, out_w = weights
    seqs, length = seg.shape
    inv_rms = lax.rsqrt(lax.optimization_barrier(jnp.mean(resid * resid, axis=-1, keepdims=True)) + EPSILON)
    normed_in = low(resid * inv_rms * gain_in)
    gate_pre = low_back(matmul(normed_in, gate_w))
    value_pre = low_back(matmul(normed_in, value_w))
    state_pre = low_back(matmul(normed_in, state_w))
    step_raw = low_back(matmul(normed_in, step_w))
    pre_conv = jnp.concatenate([value_pre, state_pre], axis=-1)
    filters = jnp.concatenate([value_filt, state_filt], axis=-1)
    offsets = jnp.concatenate([value_off, state_off], axis=-1)
    conv_sum = jnp.zeros_like(pre_conv) + offsets
    for offset in range(CONV):
        lag = CONV - 1 - offset
        moved = jnp.pad(pre_conv, ((0, 0), (lag, 0), (0, 0)))[:, :length]
        moved_seg = jnp.pad(seg, ((0, 0), (lag, 0)), constant_values=-1)[:, :length]
        conv_sum = conv_sum + filters[offset] * jnp.where((moved_seg == seg)[..., None], moved, 0.0)
    activated = jax.nn.silu(conv_sum)
    values = low(activated[..., :INNER])
    write_vec = low(activated[..., INNER:INNER + STATE])
    read_vec = low(activated[..., INNER + STATE:])
    steps = jax.nn.softplus(step_raw + bias_step)
    log_decay = -jnp.exp(decay_param) * steps
    head_vals = values.reshape(seqs, length, HEADS, HEADDIM)
    scan_out = ssd(head_vals, write_vec, read_vec, steps, log_decay, seg)
    ssm_out = low_back(scan_out + skip_param[:, None] * head_vals).reshape(seqs, length, INNER)
    gated = ssm_out * jax.nn.silu(gate_pre)
    inv_norm = lax.rsqrt(lax.optimization_barrier(jnp.sum(gated * gated, axis=-1, keepdims=True)) / INNER + EPSILON)
    out_in = low(gated * gain_out)
    branch = low_back(matmul(out_in, out_w))
    return resid + inv_norm * branch

def reference(tokens, segments, in_gain, gate_weight, value_weight, state_weight, step_weight, value_filter, value_offset, state_filter, state_offset, step_bias, decay_log, skip_gain, out_gain, out_weight, cotangent):
    seg = segments.reshape(SEQS, SEQ_LEN).astype(jnp.int32)
    start = tokens.astype(jnp.float32).reshape(SEQS, SEQ_LEN, D)
    upstream = cotangent.astype(jnp.float32).reshape(SEQS, SEQ_LEN, D)
    params = (in_gain, gate_weight, value_weight, state_weight, step_weight, value_filter, value_offset, state_filter, state_offset, step_bias, decay_log, skip_gain, out_gain, out_weight)
    params = tuple((param.astype(jnp.float32) for param in params))

    def forward(resid, weights):
        for depth in range(LAYERS):
            resid = layer_forward(resid, seg, tuple((weight[depth] for weight in weights)))
        return resid
    result, pull = jax.vjp(forward, start, params)
    grad_start, grads = pull(upstream)
    return (result.reshape(TOKENS, D).astype(jnp.bfloat16), grad_start.reshape(TOKENS, D).astype(jnp.bfloat16), grads[0], grads[1], grads[2], grads[3], grads[4], grads[5], grads[6], grads[7], grads[8], grads[9], grads[10], grads[11], grads[12], grads[13])
```

```python
import functools

import jax
import jax.numpy as jnp
from jax import lax
from jax.experimental import pallas as pl
from jax.experimental.pallas import tpu as pltpu
from jax.sharding import PartitionSpec as P

CONV = 4
GROUP = 256
LAYERS = 2
INNER = 1536
EDGE = 8
LANES = 128


EPSILON = 1e-05
PRECISE = lax.Precision.HIGHEST
FLOAT = jnp.float32
BFLOAT = jnp.bfloat16
VMEM_BYTES = 56 * 1024 * 1024


def nn(left, right, precision=None):
    return lax.dot_general(
        left, right, (((1,), (0,)), ((), ())), precision=precision, preferred_element_type=FLOAT
    )


def nt(left, right, precision=None):
    return lax.dot_general(
        left, right, (((1,), (1,)), ((), ())), precision=precision, preferred_element_type=FLOAT
    )


def tn(left, right, precision=None):
    return lax.dot_general(
        left, right, (((0,), (0,)), ((), ())), precision=precision, preferred_element_type=FLOAT
    )


def sigmoid(value):
    return 1.0 / (1.0 + jnp.exp(-value))


def softplus(value):
    small = jnp.exp(-jnp.abs(value))
    series = small * (1.0 - small * (0.5 - small * (1.0 / 3.0 - small * 0.25)))
    return jnp.maximum(value, 0.0) + jnp.where(small < 0.01, series, jnp.log(1.0 + small))


def silu_slope(value):
    sigma = sigmoid(value)
    return sigma * (1.0 + value * (1.0 - sigma))


def spread_matrix(lane_count, heads):
    size = lane_count // heads
    head = lax.broadcasted_iota(jnp.int32, (LANES, lane_count), 0)
    lane = lax.broadcasted_iota(jnp.int32, (LANES, lane_count), 1)
    return jnp.where((lane >= head * size) & (lane < (head + 1) * size), 1.0, 0.0).astype(FLOAT)


def triangle(span, upper):
    row = lax.broadcasted_iota(jnp.int32, (span, span), 0)
    col = lax.broadcasted_iota(jnp.int32, (span, span), 1)
    return jnp.where(col >= row if upper else col <= row, 1.0, 0.0).astype(FLOAT)


def within_block(seg_col, seg_row):
    span = seg_col.shape[0]
    row = lax.broadcasted_iota(jnp.int32, (span, span), 0)
    col = lax.broadcasted_iota(jnp.int32, (span, span), 1)
    return (row >= col) & (seg_col == seg_row)


def call(body, grid, inputs, outputs, scratch=(), reverse=False, flops=0):
    def place(b):
        return grid - 1 - b if reverse else b

    def spec_of(shape, kind):
        if isinstance(kind, pl.BlockSpec):
            return kind
        if kind == "smem":
            return pl.BlockSpec(memory_space=pltpu.SMEM)
        if kind == "rows":
            return pl.BlockSpec((shape[0] // grid, shape[1]), lambda b: (place(b), 0))
        if kind == "lead":
            return pl.BlockSpec((None,) + tuple(shape[1:]), lambda b: (place(b),) + (0,) * (len(shape) - 1))
        return pl.BlockSpec(tuple(shape), lambda b: (0,) * len(shape))

    moved = sum(a.size * a.dtype.itemsize for a, _ in inputs)
    return pl.pallas_call(
        body,
        grid=(grid,),
        in_specs=[spec_of(a.shape, kind) for a, kind in inputs],
        out_specs=[spec_of(shape, kind) for shape, _, kind in outputs],
        out_shape=[jax.ShapeDtypeStruct(shape, dtype) for shape, dtype, _ in outputs],
        scratch_shapes=list(scratch),
        compiler_params=pltpu.CompilerParams(
            dimension_semantics=("arbitrary",), vmem_limit_bytes=VMEM_BYTES
        ),
        cost_estimate=pl.CostEstimate(flops=int(flops), bytes_accessed=int(2 * moved), transcendentals=0),
    )(*[a for a, _ in inputs])


def project_kernel(
    resid, halo, gain, gate_w, value_w, state_w, step_w, filt, off, bias, rate, meta,
    normed_o, gate_o, pre_o, pre_halo_o, conv_o, vals_o, wr_o, shifted_o, cum_o, local_o, retain_o, pay_o,
    ext, state,
):
    b = pl.program_id(0)
    span = resid.shape[0]
    lanes = value_w.shape[1]
    heads_rows = state.shape[0]

    def normalise(x):
        x = x.astype(FLOAT)
        inv = lax.rsqrt(jnp.mean(x * x, axis=1, keepdims=True) + EPSILON)
        return (x * inv * gain[...]).astype(BFLOAT)

    @pl.when(b == 0)
    def _():
        edge = normalise(halo[...])
        edge_pre = jnp.concatenate([nn(edge, value_w[...]), nn(edge, state_w[...])], axis=1)
        ext[0:EDGE] = edge_pre
        pre_halo_o[...] = edge_pre
        state[...] = jnp.zeros_like(state)

    @pl.when(b > 0)
    def _():
        ext[0:EDGE] = ext[span : span + EDGE]

    normed = normalise(resid[...])
    normed_o[...] = normed
    gate_o[...] = nn(normed, gate_w[...])
    ext[EDGE : span + EDGE, 0:lanes] = nn(normed, value_w[...])
    ext[EDGE : span + EDGE, lanes:] = nn(normed, state_w[...])
    pre = ext[EDGE : span + EDGE]
    pre_o[...] = pre
    conv_sum = off[...] + filt[CONV - 1 : CONV] * pre
    for k in range(CONV - 1):
        at = EDGE - (CONV - 1) + k
        conv_sum = conv_sum + filt[k : k + 1] * (ext[at : at + span] * meta[:, k : k + 1])
    conv_o[...] = conv_sum
    activated = conv_sum * sigmoid(conv_sum)
    vals = activated[:, :lanes].astype(BFLOAT)
    write_read = activated[:, lanes:].astype(BFLOAT)
    vals_o[...] = vals
    wr_o[...] = write_read
    write = write_read[:, : write_read.shape[1] // 2]

    shifted = nn(normed, step_w[...]) + bias[...]
    shifted_o[...] = shifted
    steps = softplus(shifted)
    log_decay = -rate[...] * steps
    cum = nn(triangle(span, False), log_decay, PRECISE)
    cum_o[...] = cum
    last = cum[span - 1 : span]
    tail_step = meta[:, 4:5] * jnp.exp(last - cum) * steps
    heads = HEADS_OF(lanes)
    spread = spread_matrix(lanes, heads)
    weight = nn(tail_step, spread, PRECISE)
    local = tn((weight * vals.astype(FLOAT)).astype(BFLOAT), write)
    retain = meta[span - 1 : span, 3:4] * jnp.exp(last)
    retain_o[...] = jnp.broadcast_to(retain, retain_o.shape)
    size = heads_rows // heads
    local_o[...] = state[...]

    @pl.when(b == 0)
    def _():
        pay_o[heads_rows:] = jnp.ones_like(pay_o[heads_rows:])

    for h in range(heads):
        rows = slice(h * size, (h + 1) * size)
        state[rows] = retain[:, h : h + 1] * state[rows] + local[rows]
    pay_o[0:heads_rows] = state[...]
    pay_o[heads_rows:] = pay_o[heads_rows:] * retain


def HEADS_OF(lanes):
    return lanes // 64


def inside_kernel(vals, wr, cum, shifted, meta, seg_row, y_o):
    lanes = vals.shape[1]
    heads = HEADS_OF(lanes)
    size = lanes // heads
    half = wr.shape[1] // 2
    mask = within_block(meta[:, 5:6], seg_row[...])
    mixed = jnp.where(mask, nt(wr[:, half:], wr[:, :half]), 0.0)
    cum_v = cum[...]
    cum_t = cum_v.T
    step_t = softplus(shifted[...]).T
    for h in range(heads):
        gap = jnp.where(mask, cum_v[:, h : h + 1] - cum_t[h : h + 1, :], 0.0)
        mixing = (mixed * jnp.exp(gap) * step_t[h : h + 1, :]).astype(BFLOAT)
        y_o[:, h * size : (h + 1) * size] = nn(mixing, vals[:, h * size : (h + 1) * size])


def fold_in(me, count, payload, acc, reverse, heads):
    rows = acc.shape[0]
    size = rows // heads
    acc[...] = jnp.zeros_like(acc)
    for k in range(count):
        at = count - 1 - k if reverse else k
        reached = at > me if reverse else at < me

        @pl.when(reached)
        def _():
            keep = payload[at, rows : rows + 1]
            for h in range(heads):
                part = slice(h * size, (h + 1) * size)
                acc[part] = keep[:, h : h + 1] * acc[part] + payload[at, part]


def gated_kernel(
    me, payload, local, retain, y, wr, vals, cum, meta, gate, skip, gain, out_w, *rest, last_layer
):
    if last_layer:
        cot, ssm_o, states_o, partial_o, sq_o, dot_o, acc = rest
    else:
        ssm_o, states_o, partial_o, sq_o, acc = rest
    b = pl.program_id(0)
    lanes = vals.shape[1]
    heads = HEADS_OF(lanes)
    rows = acc.shape[0]
    size = rows // heads
    half = wr.shape[1] // 2

    @pl.when(b == 0)
    def _():
        fold_in(me[0], payload.shape[0], payload, acc, False, heads)

    states = local[...] + acc[...]
    states_o[...] = states
    for h in range(heads):
        part = slice(h * size, (h + 1) * size)
        acc[part] = retain[0:1, h : h + 1] * acc[part]
    enter = meta[:, 3:4] * jnp.exp(cum[...])
    enter_lanes = nn(enter, spread_matrix(lanes, heads), PRECISE)
    carried = nt(wr[:, half:], states.astype(BFLOAT)) * enter_lanes
    ssm = y[...] + carried + skip[...] * vals[...].astype(FLOAT)
    ssm_o[...] = ssm
    gate_v = gate[...]
    gated = ssm * (gate_v * sigmoid(gate_v))
    partial = nn((gated * gain[...]).astype(BFLOAT), out_w[...])
    partial_o[...] = partial
    ones = jnp.ones((8, lanes), FLOAT)
    sq_o[...] = nt(ones, gated * gated, PRECISE)[0:1]
    if last_layer:
        ones = jnp.ones((8, partial.shape[1]), FLOAT)
        dot_o[...] = nt(ones, partial * cot[...].astype(FLOAT), PRECISE)[0:1]


def ungate_kernel(
    upstream, cols, out_w, gain, gate, ssm, vals, wr, cum, meta, retain,
    grad_ssm_o, gate_low_o, grad_out_w_o, small_o, later_o, pay_o,
    state,
):
    b = pl.program_id(0)
    lanes = vals.shape[1]
    heads = HEADS_OF(lanes)
    rows = state.shape[0]
    size = rows // heads
    half = wr.shape[1] // 2

    @pl.when(b == 0)
    def _():
        state[...] = jnp.zeros_like(state)
        grad_out_w_o[...] = jnp.zeros_like(grad_out_w_o)
        small_o[...] = jnp.zeros_like(small_o)
        pay_o[rows:] = jnp.ones_like(pay_o[rows:])

    inv_norm = cols[:, 0:1]
    grad_branch = (inv_norm * upstream[...].astype(FLOAT)).astype(BFLOAT)
    gate_v = gate[...]
    sigma = sigmoid(gate_v)
    gate_act = gate_v * sigma
    ssm_v = ssm[...]
    gated = ssm_v * gate_act
    out_in = (gated * gain[...]).astype(BFLOAT)
    grad_out_w_o[...] += tn(out_in, grad_branch)
    grad_out_in = nt(grad_branch, out_w[...])
    small_o[0:1] += jnp.sum(grad_out_in * gated, axis=0, keepdims=True)
    grad_gated = grad_out_in * gain[...] - (cols[:, 1:2] * inv_norm * inv_norm * inv_norm / INNER) * gated
    grad_ssm = (grad_gated * gate_act).astype(BFLOAT)
    grad_ssm_o[...] = grad_ssm
    gate_low_o[...] = (grad_gated * ssm_v * (sigma * (1.0 + gate_v * (1.0 - sigma)))).astype(BFLOAT)
    grad_wide = grad_ssm.astype(FLOAT)
    small_o[1:2] += jnp.sum(grad_wide * vals[...].astype(FLOAT), axis=0, keepdims=True)
    enter = meta[:, 3:4] * jnp.exp(cum[...])
    enter_lanes = nn(enter, spread_matrix(lanes, heads), PRECISE)
    pulls = tn((enter_lanes * grad_wide).astype(BFLOAT), wr[:, half:])
    later_o[...] = state[...]
    keep = retain[0:1]
    for h in range(heads):
        part = slice(h * size, (h + 1) * size)
        state[part] = keep[:, h : h + 1] * state[part] + pulls[part]
    pay_o[0:rows] = state[...]
    pay_o[rows:] = pay_o[rows:] * keep


def unmix_kernel(
    me, payload, later, retain, grad_ssm, vals, wr, cum, shifted, meta, seg_row, states, conv, pre, before, pre_halo,
    filt, rate, skip,
    low_o, edge_o, step_low_o, spill_o, small_o, small2_o,
    acc, flows, ext,
):
    b = pl.program_id(0)
    blocks = pl.num_programs(0)
    span, lanes = vals.shape
    heads = HEADS_OF(lanes)
    rows = acc.shape[0]
    size = rows // heads
    half = wr.shape[1] // 2
    write, read = wr[:, :half], wr[:, half:]

    @pl.when(b == 0)
    def _():
        fold_in(me[0], payload.shape[0], payload, acc, True, heads)
        small_o[...] = jnp.zeros_like(small_o)
        small2_o[...] = jnp.zeros_like(small2_o)
        for k in range(CONV - 1):
            ext[k, span:] = jnp.zeros_like(ext[k, span:])

    @pl.when(b > 0)
    def _():
        for k in range(CONV - 1):
            ext[k, span:] = ext[k, 0:EDGE]

    grad_next = later[...] + acc[...]
    keep = retain[0:1]
    states_v = states[...]
    spread = spread_matrix(lanes, heads)
    meet = jnp.sum(grad_next * states_v, axis=1, keepdims=True)
    grad_retain = tn(jnp.broadcast_to(meet, (rows, LANES)) * spread.T, jnp.ones((rows, 8), FLOAT), PRECISE)
    grad_retain = grad_retain.T[0:1]
    for h in range(heads):
        part = slice(h * size, (h + 1) * size)
        acc[part] = keep[:, h : h + 1] * acc[part]

    cum_v = cum[...]
    cum_t = cum_v.T
    shifted_v = shifted[...]
    steps = softplus(shifted_v)
    step_t = steps.T
    seg_mask = within_block(meta[:, 5:6], seg_row[...])
    inter = jnp.where(seg_mask, nt(read, write), 0.0)
    grad_inter = jnp.zeros((span, span), FLOAT)
    flows[...] = jnp.zeros_like(flows)
    parts = []
    row_sums = jnp.zeros((span, LANES), FLOAT)
    lane_no = lax.broadcasted_iota(jnp.int32, (span, LANES), 1)
    for h in range(heads):
        part = slice(h * size, (h + 1) * size)
        decay = jnp.exp(jnp.where(seg_mask, cum_v[:, h : h + 1] - cum_t[h : h + 1, :], 0.0))
        decay_inter = decay * inter
        step_h = step_t[h : h + 1, :]
        mixing = (decay_inter * step_h).astype(BFLOAT)
        grad_h = grad_ssm[:, part]
        parts.append(tn(mixing, grad_h))
        pairing = nt(grad_h, vals[:, part])
        grad_inter = grad_inter + pairing * decay * step_h
        weighted = pairing * decay_inter
        col = jnp.sum(weighted, axis=0, keepdims=True)
        flows[h : h + 1, :] = col
        row_sums = row_sums + jnp.where(
            lane_no == h, jnp.sum(weighted * step_h, axis=1, keepdims=True), 0.0
        )
    grad_vals = jnp.concatenate(parts, axis=1)
    grad_steps = flows[...].T
    grad_cum = row_sums - grad_steps * steps
    grad_inter = jnp.where(seg_mask, grad_inter, 0.0).astype(BFLOAT)
    grad_read = nn(grad_inter, write)
    grad_write = tn(grad_inter, read)

    vals_f = vals[...].astype(FLOAT)
    grad_f = grad_ssm[...].astype(FLOAT)
    enter = meta[:, 3:4] * jnp.exp(cum_v)
    enter_lanes = nn(enter, spread, PRECISE)
    states_low = states_v.astype(BFLOAT)
    grad_read = grad_read + nn((enter_lanes * grad_f).astype(BFLOAT), states_low)
    out_of = nt(read, states_low)
    grad_cum = grad_cum + enter * nt(grad_f * out_of, spread, PRECISE)
    next_low = grad_next.astype(BFLOAT)
    along = nt(write, next_low)
    last = cum_v[span - 1 : span]
    tail = meta[:, 4:5] * jnp.exp(last - cum_v)
    tail_step = tail * steps
    tail_lanes = nn(tail_step, spread, PRECISE)
    grad_vals = grad_vals + tail_lanes * along + skip[...] * grad_f
    grad_write = grad_write + nn((tail_lanes * vals_f).astype(BFLOAT), next_low)
    reach = nt(vals_f * along, spread, PRECISE)
    grad_steps = grad_steps + tail * reach
    tail_flow = tail_step * reach
    grad_last = jnp.sum(tail_flow, axis=0, keepdims=True) + grad_retain * keep
    grad_log = nn(triangle(span, True), grad_cum - tail_flow, PRECISE) + grad_last
    rate_v = rate[...]
    log_decay = -rate_v * steps
    small2_o[0:1] += jnp.sum(grad_log * log_decay, axis=0, keepdims=True)
    grad_shifted = (grad_steps - rate_v * grad_log) * sigmoid(shifted_v)
    small2_o[1:2] += jnp.sum(grad_shifted, axis=0, keepdims=True)
    step_low_o[...] = grad_shifted.astype(BFLOAT)

    grad_conv = jnp.concatenate([grad_vals, grad_write, grad_read], axis=1) * silu_slope(conv[...])
    small_o[CONV : CONV + 1] += jnp.sum(grad_conv, axis=0, keepdims=True)
    pre_v = pre[...]
    small_o[CONV - 1 : CONV] += jnp.sum(grad_conv * pre_v, axis=0, keepdims=True)
    grad_pre = filt[CONV - 1 : CONV] * grad_conv
    first = blocks - 1 - b == 0
    for k in range(CONV - 1):
        lag = CONV - 1 - k
        masked = grad_conv * meta[:, k : k + 1]
        ext[k, 0:span] = masked
        ahead = ext[k, lag : lag + span]
        row_no = lax.broadcasted_iota(jnp.int32, (span, 1), 0)
        own = jnp.where(row_no < span - lag, ahead, 0.0)
        edge = jnp.where(first, pre_halo[...], before[...])
        head_rows = ext[k, 0:EDGE]
        edge_sum = jnp.zeros((1, head_rows.shape[1]), FLOAT)
        for t in range(lag):
            edge_sum = edge_sum + head_rows[t : t + 1] * edge[EDGE - lag + t : EDGE - lag + t + 1]
        small_o[k : k + 1] += jnp.sum(own * pre_v, axis=0, keepdims=True) + edge_sum
        grad_pre = grad_pre + filt[k : k + 1] * ahead
    low_o[...] = grad_pre.astype(BFLOAT)

    @pl.when(b == 0)
    def _():
        edge_o[...] = grad_pre[span - EDGE :]

    spill_o[...] = jnp.zeros_like(spill_o)
    for k in range(CONV - 1):
        lag = CONV - 1 - k
        for t in range(lag):
            at = EDGE - lag + t
            spill_o[at : at + 1] += filt[k : k + 1] * ext[k, t : t + 1]


def weights_kernel(
    normed, low, edge, spill, gate_low, step_low, gate_w, value_w, state_w, step_w,
    grad_normed_o, gate_o, value_o, state_o, step_o,
):
    b = pl.program_id(0)
    blocks = pl.num_programs(0)
    span = low.shape[0]
    lanes = value_w.shape[1]

    @pl.when(b == 0)
    def _():
        gate_o[...] = jnp.zeros_like(gate_o)
        value_o[...] = jnp.zeros_like(value_o)
        state_o[...] = jnp.zeros_like(state_o)
        step_o[...] = jnp.zeros_like(step_o)

    patch = (edge[...] + spill[...]).astype(FLOAT)
    padded = jnp.concatenate([jnp.zeros((span - EDGE, patch.shape[1]), FLOAT), patch], axis=0)
    row_no = lax.broadcasted_iota(jnp.int32, (span, 1), 0)
    use = (row_no >= span - EDGE) & (b == blocks - 1)
    low_v = jnp.where(use, padded, low[...].astype(FLOAT)).astype(BFLOAT)
    value_low, state_low = low_v[:, :lanes], low_v[:, lanes:]
    normed_v = normed[...]
    gate_o[...] += tn(normed_v, gate_low[...])
    value_o[...] += tn(normed_v, value_low)
    state_o[...] += tn(normed_v, state_low)
    step_o[...] += tn(normed_v, step_low[...])
    grad_normed_o[...] = (
        nt(gate_low[...], gate_w[...])
        + nt(value_low, value_w[...])
        + nt(state_low, state_w[...])
        + nt(step_low[...], step_w[...])
    )


def passed_along(shard, axis, by):
    count = lax.axis_size(axis)
    pairs = [(i, i + by) for i in range(count) if 0 <= i + by < count]
    return lax.ppermute(shard, axis, pairs)


def pad_lanes(array):
    return jnp.pad(array, ((0, 0), (0, LANES - array.shape[1])))


def prepare(params):
    (
        gain_in, gate_w, value_w, state_w, step_w, value_filt, value_off, state_filt, state_off,
        bias_step, decay_param, skip_param, gain_out, out_w,
    ) = params
    heads = step_w.shape[1]
    size = value_w.shape[1] // heads
    filt = jnp.concatenate([value_filt, state_filt], axis=1)
    return dict(
        gain=gain_in[None],
        gate_w=gate_w,
        value_w=value_w,
        state_w=state_w,
        step_w=pad_lanes(step_w),
        filt=jnp.pad(filt, ((0, 8 - CONV), (0, 0))),
        off=jnp.concatenate([value_off, state_off])[None],
        bias=pad_lanes(bias_step[None]),
        rate=pad_lanes(jnp.exp(decay_param)[None]),
        skip=jnp.repeat(skip_param, size)[None],
        gain_out=gain_out[None],
        out_w=out_w,
    )


def forward_layer(resid, halo, w, geometry, me, cot):
    meta, seg_row = geometry
    n, d = resid.shape
    grid = n // GROUP
    lanes = w["value_w"].shape[1]
    chans = lanes + w["state_w"].shape[1]
    state = w["state_w"].shape[1] // 2
    pay = (lanes + 8, state)
    normed, gate, pre, pre_halo, conv, vals, wr, shifted, cum, local, retain, payload = call(
        project_kernel, grid,
        [
            (resid, "rows"), (halo, "whole"), (w["gain"], "whole"), (w["gate_w"], "whole"),
            (w["value_w"], "whole"), (w["state_w"], "whole"), (w["step_w"], "whole"), (w["filt"], "whole"),
            (w["off"], "whole"), (w["bias"], "whole"), (w["rate"], "whole"), (meta, "rows"),
        ],
        [
            ((n, d), BFLOAT, "rows"), ((n, lanes), FLOAT, "rows"), ((n, chans), FLOAT, "rows"),
            ((EDGE, chans), FLOAT, "whole"), ((n, chans), FLOAT, "rows"), ((n, lanes), BFLOAT, "rows"),
            ((n, chans - lanes), BFLOAT, "rows"), ((n, LANES), FLOAT, "rows"), ((n, LANES), FLOAT, "rows"),
            ((grid, lanes, state), FLOAT, "lead"), ((grid, 8, LANES), FLOAT, "lead"), (pay, FLOAT, "whole"),
        ],
        [pltpu.VMEM((GROUP + EDGE, chans), FLOAT), pltpu.VMEM((lanes, state), FLOAT)],
        flops=2 * n * d * (lanes + chans),
    )
    everything = lax.all_gather(payload, "ctx")
    (y,) = call(
        inside_kernel, grid,
        [(vals, "rows"), (wr, "rows"), (cum, "rows"), (shifted, "rows"), (meta, "rows"), (seg_row, "lead")],
        [((n, lanes), FLOAT, "rows")],
        flops=4 * n * GROUP * lanes,
    )
    row = ((grid, 1, GROUP), FLOAT, "lead")
    outs = call(
        functools.partial(gated_kernel, last_layer=cot is not None), grid,
        [
            (me, "smem"), (everything, "whole"), (local, "lead"), (retain, "lead"), (y, "rows"), (wr, "rows"),
            (vals, "rows"), (cum, "rows"), (meta, "rows"), (gate, "rows"), (w["skip"], "whole"),
            (w["gain_out"], "whole"), (w["out_w"], "whole"),
        ] + ([(cot, "rows")] if cot is not None else []),
        [
            ((n, lanes), FLOAT, "rows"), ((grid, lanes, state), FLOAT, "lead"), ((n, d), FLOAT, "rows"), row,
        ] + ([row] if cot is not None else []),
        [pltpu.VMEM((lanes, state), FLOAT)],
        flops=2 * n * d * lanes,
    )
    ssm, states = outs[0], outs[1]
    saved = (normed, gate, pre, pre_halo, conv, vals, wr, shifted, cum, retain, ssm, states)
    return outs[2:], saved


def backward_layer(upstream, cols, w, saved, geometry, me):
    meta, seg_row = geometry
    normed, gate, pre, pre_halo, conv, vals, wr, shifted, cum, retain, ssm, states = saved
    n, d = upstream.shape
    grid = n // GROUP
    lanes = vals.shape[1]
    chans = pre.shape[1]
    state = wr.shape[1] // 2
    pay = (lanes + 8, state)
    grad_ssm, gate_low, grad_out_w, small, later, payload = call(
        ungate_kernel, grid,
        [
            (upstream, "rows"), (cols, "rows"), (w["out_w"], "whole"), (w["gain_out"], "whole"), (gate, "rows"),
            (ssm, "rows"), (vals, "rows"), (wr, "rows"), (cum, "rows"), (meta, "rows"), (retain, "lead"),
        ],
        [
            ((n, lanes), BFLOAT, "rows"), ((n, lanes), BFLOAT, "rows"), ((lanes, d), FLOAT, "whole"),
            ((8, lanes), FLOAT, "whole"), ((grid, lanes, state), FLOAT, "lead"), (pay, FLOAT, "whole"),
        ],
        [pltpu.VMEM((lanes, state), FLOAT)],
        reverse=True,
        flops=4 * n * d * lanes,
    )
    everything = lax.all_gather(payload, "ctx")
    strip = GROUP // EDGE
    before = pl.BlockSpec((EDGE, chans), lambda b: (jnp.maximum((grid - 1 - b) * strip - 1, 0), 0))
    low, edge, step_low, spill, small_c, small_h = call(
        unmix_kernel, grid,
        [
            (me, "smem"), (everything, "whole"), (later, "lead"), (retain, "lead"), (grad_ssm, "rows"),
            (vals, "rows"), (wr, "rows"), (cum, "rows"), (shifted, "rows"), (meta, "rows"), (seg_row, "lead"),
            (states, "lead"), (conv, "rows"), (pre, "rows"), (pre, before), (pre_halo, "whole"),
            (w["filt"], "whole"), (w["rate"], "whole"), (w["skip"], "whole"),
        ],
        [
            ((n, chans), BFLOAT, "rows"), ((EDGE, chans), FLOAT, "whole"), ((n, LANES), BFLOAT, "rows"),
            ((EDGE, chans), FLOAT, "whole"), ((8, chans), FLOAT, "whole"), ((8, LANES), FLOAT, "whole"),
        ],
        [
            pltpu.VMEM((lanes, state), FLOAT), pltpu.VMEM((LANES, GROUP), FLOAT),
            pltpu.VMEM((CONV - 1, GROUP + EDGE, chans), FLOAT),
        ],
        reverse=True,
        flops=12 * n * GROUP * lanes,
    )
    spill = passed_along(spill, "ctx", -1)
    grad_normed, grad_gate_w, grad_value_w, grad_state_w, grad_step_w = call(
        weights_kernel, grid,
        [
            (normed, "rows"), (low, "rows"), (edge, "whole"), (spill, "whole"), (gate_low, "rows"),
            (step_low, "rows"), (w["gate_w"], "whole"), (w["value_w"], "whole"), (w["state_w"], "whole"),
            (w["step_w"], "whole"),
        ],
        [
            ((n, d), FLOAT, "rows"), ((d, lanes), FLOAT, "whole"), ((d, lanes), FLOAT, "whole"),
            ((d, chans - lanes), FLOAT, "whole"), ((d, LANES), FLOAT, "whole"),
        ],
        flops=4 * n * d * (lanes + chans),
    )
    heads = HEADS_OF(lanes)
    grads = dict(
        gate=grad_gate_w,
        value=grad_value_w,
        state=grad_state_w,
        step=grad_step_w[:, :heads],
        value_filter=small_c[:CONV, :lanes],
        value_offset=small_c[CONV, :lanes],
        state_filter=small_c[:CONV, lanes:],
        state_offset=small_c[CONV, lanes:],
        bias=small_h[1, :heads],
        decay=small_h[0, :heads],
        skip=jnp.sum(small[1].reshape(heads, -1), axis=1),
        gain_out=small[0],
        out=grad_out_w,
    )
    return grad_normed, grads


def total_over(grads, gain_in):
    every = ("dp", "ctx", "tensor")
    wide = lax.psum((grads["gate"], grads["value"], grads["out"]), ("dp", "ctx"))
    state = lax.psum((grads["state"], grads["state_filter"], grads["state_offset"]), every)
    rest = ("step", "value_filter", "value_offset", "bias", "decay", "skip", "gain_out")
    others = lax.psum((gain_in,) + tuple(grads[name] for name in rest), ("dp", "ctx"))
    return (
        others[0], wide[0], wide[1], state[0], others[1], others[2], others[3], state[1], state[2],
        others[4], others[5], others[6], others[7], wide[2],
    )


def local(tokens, segments, *rest):
    params, cotangent = rest[:-1], rest[-1]
    n = tokens.shape[0]
    me = lax.axis_index("ctx").astype(jnp.int32).reshape(1)
    halo = passed_along(tokens[n - EDGE :].astype(FLOAT), "ctx", 1)
    halo_seg = passed_along(segments[n - EDGE :], "ctx", 1)
    seg_ext = jnp.concatenate([halo_seg, segments])
    seg_blocks = segments.reshape(-1, GROUP)
    seg_before = jnp.concatenate([halo_seg[EDGE - 1 :], seg_blocks[:-1, -1]])
    first = EDGE - (CONV - 1)
    columns = [seg_ext[first + k : first + k + n] == segments for k in range(CONV - 1)]
    columns.append((seg_blocks == seg_before[:, None]).reshape(n))
    columns.append((seg_blocks == seg_blocks[:, -1:]).reshape(n))
    columns.append(segments)
    columns += [jnp.zeros_like(segments)] * (8 - len(columns))
    meta = jnp.stack([column.astype(FLOAT) for column in columns], axis=1)
    geometry = (meta, segments.astype(FLOAT).reshape(-1, 1, GROUP))
    weights = [prepare(tuple(param[depth] for param in params)) for depth in range(LAYERS)]

    resid = tokens.astype(FLOAT)
    entering, saved_all, norms = [resid], [], []
    for depth in range(LAYERS - 1):
        (partial, squares), saved = forward_layer(resid, halo, weights[depth], geometry, me, None)
        saved_all.append(saved)
        branch, total_sq = lax.psum((partial, squares.reshape(n)), "tensor")
        inv_norm = lax.rsqrt(total_sq / INNER + EPSILON)[:, None]
        norms.append((inv_norm, branch))
        resid = resid + inv_norm * branch
        entering.append(resid)
        halo = passed_along(resid[n - EDGE :], "ctx", 1)
    (partial, squares, dots), saved = forward_layer(
        resid, halo, weights[LAYERS - 1], geometry, me, cotangent
    )
    saved_all.append(saved)
    total_sq, grad_inv = lax.psum((squares, dots), "tensor")
    inv_norm = lax.rsqrt(total_sq.reshape(n) / INNER + EPSILON)[:, None]
    grad_inv = grad_inv.reshape(n)[:, None]
    branch = lax.psum(partial, "tensor")
    mixed = (resid + inv_norm * branch).astype(BFLOAT)

    upstream = cotangent.astype(FLOAT)
    layer_grads = [None] * LAYERS
    for depth in range(LAYERS - 1, -1, -1):
        if depth < LAYERS - 1:
            inv_norm, branch = norms[depth]
            grad_inv = jnp.sum(upstream * branch, axis=1, keepdims=True)
        cols = jnp.concatenate([inv_norm, grad_inv, jnp.zeros((n, 6), FLOAT)], axis=1)
        grad_normed, grads = backward_layer(upstream, cols, weights[depth], saved_all[depth], geometry, me)
        grad_normed = lax.psum(grad_normed, "tensor")
        x = entering[depth]
        inv_rms = lax.rsqrt(jnp.mean(x * x, axis=1, keepdims=True) + EPSILON)
        scaled = x * inv_rms
        gain_grad = jnp.sum(grad_normed * scaled, axis=0)
        inner = grad_normed * weights[depth]["gain"]
        upstream = upstream + inv_rms * (inner - scaled * jnp.mean(inner * scaled, axis=1, keepdims=True))
        layer_grads[depth] = total_over(grads, gain_grad)
    stacked = [jnp.stack([layer_grads[depth][i] for depth in range(LAYERS)]) for i in range(14)]
    return (mixed, upstream.astype(BFLOAT), *stacked)


def solution(mesh):
    split = P(None, None, "tensor")
    lane = P(None, "tensor")
    rows = P(("dp", "ctx"), None)
    weights = (P(), split, split, P(), split, split, lane, P(), P(), lane, lane, lane, lane, P(None, "tensor", None))
    return jax.shard_map(
        local,
        mesh=mesh,
        in_specs=(rows, P(("dp", "ctx")), *weights, rows),
        out_specs=(rows, rows, *weights),
        check_vma=False,
    )
```

```python
import functools

import jax
import jax.numpy as jnp
from jax import lax
from jax.experimental import pallas as pl
from jax.experimental.pallas import tpu as pltpu
from jax.sharding import PartitionSpec as P

CONV = 4
GROUP = 256
LAYERS = 2
INNER = 1536
EDGE = 8
LANES = 128


EPSILON = 1e-05
PRECISE = lax.Precision.HIGHEST
FLOAT = jnp.float32
BFLOAT = jnp.bfloat16
VMEM_BYTES = 56 * 1024 * 1024


def nn(left, right, precision=None):
    return lax.dot_general(
        left, right, (((1,), (0,)), ((), ())), precision=precision, preferred_element_type=FLOAT
    )


def nt(left, right, precision=None):
    return lax.dot_general(
        left, right, (((1,), (1,)), ((), ())), precision=precision, preferred_element_type=FLOAT
    )


def tn(left, right, precision=None):
    return lax.dot_general(
        left, right, (((0,), (0,)), ((), ())), precision=precision, preferred_element_type=FLOAT
    )


def sigmoid(value):
    return 1.0 / (1.0 + jnp.exp(-value))


def softplus(value):
    small = jnp.exp(-jnp.abs(value))
    series = small * (1.0 - small * (0.5 - small * (1.0 / 3.0 - small * 0.25)))
    return jnp.maximum(value, 0.0) + jnp.where(small < 0.01, series, jnp.log(1.0 + small))


def silu_slope(value):
    sigma = sigmoid(value)
    return sigma * (1.0 + value * (1.0 - sigma))


def spread_matrix(lane_count, heads):
    size = lane_count // heads
    head = lax.broadcasted_iota(jnp.int32, (LANES, lane_count), 0)
    lane = lax.broadcasted_iota(jnp.int32, (LANES, lane_count), 1)
    return jnp.where((lane >= head * size) & (lane < (head + 1) * size), 1.0, 0.0).astype(FLOAT)


def triangle(span, upper):
    row = lax.broadcasted_iota(jnp.int32, (span, span), 0)
    col = lax.broadcasted_iota(jnp.int32, (span, span), 1)
    return jnp.where(col >= row if upper else col <= row, 1.0, 0.0).astype(FLOAT)


def within_block(seg_col, seg_row):
    span = seg_col.shape[0]
    row = lax.broadcasted_iota(jnp.int32, (span, span), 0)
    col = lax.broadcasted_iota(jnp.int32, (span, span), 1)
    return (row >= col) & (seg_col == seg_row)


def call(body, grid, inputs, outputs, scratch=(), reverse=False, flops=0, aliases=None, deps=()):
    def place(b):
        return grid - 1 - b if reverse else b

    def spec_of(shape, kind):
        if isinstance(kind, pl.BlockSpec):
            return kind
        if kind == "smem":
            return pl.BlockSpec(memory_space=pltpu.SMEM)
        if kind == "rows":
            return pl.BlockSpec((shape[0] // grid, shape[1]), lambda b: (place(b), 0))
        if kind == "lead":
            return pl.BlockSpec((None,) + tuple(shape[1:]), lambda b: (place(b),) + (0,) * (len(shape) - 1))
        return pl.BlockSpec(tuple(shape), lambda b: (0,) * len(shape))

    known = len(inputs)
    inputs = list(inputs) + [(dep, pl.BlockSpec(memory_space=pl.ANY)) for dep in deps]

    def run(*refs):
        body(*refs[:known], *refs[len(inputs) :])

    moved = sum(a.size * a.dtype.itemsize for a, _ in inputs)
    return pl.pallas_call(
        run,
        grid=(grid,),
        in_specs=[spec_of(a.shape, kind) for a, kind in inputs],
        out_specs=[spec_of(shape, kind) for shape, _, kind in outputs],
        out_shape=[jax.ShapeDtypeStruct(shape, dtype) for shape, dtype, _ in outputs],
        scratch_shapes=list(scratch),
        input_output_aliases=aliases or {},
        compiler_params=pltpu.CompilerParams(
            dimension_semantics=("arbitrary",), vmem_limit_bytes=VMEM_BYTES
        ),
        cost_estimate=pl.CostEstimate(flops=int(flops), bytes_accessed=int(2 * moved), transcendentals=0),
    )(*[a for a, _ in inputs])


def column(row):
    return jnp.broadcast_to(row, (8, row.shape[1])).T[:, 0:1]


def summed(b, core, mine, other):
    span = GROUP
    per = mine.shape[0] // span
    use = b // per == core
    rows = pl.ds(pl.multiple_of((b % per) * span, span), span)
    return jnp.where(use, mine[rows], other[rows]), use, b % per


def branch_of(b, core, mine, other):
    total, use, at = summed(b, core, mine, other)
    size = mine.shape[0] - EDGE
    squares = jnp.where(use, mine[size : size + 1], other[size : size + 1])
    row = squares[:, 0:GROUP]
    for k in range(1, size // GROUP):
        row = jnp.where(at == k, squares[:, k * GROUP : (k + 1) * GROUP], row)
    return total, lax.rsqrt(column(row) / INNER + EPSILON)


def project_kernel(flags, *refs, first_layer):
    if first_layer:
        (tokens, got, halo), refs = refs[:3], refs[3:]
    else:
        (resid, mine, other, halo, edge), refs = refs[:5], refs[5:]
    (
        gain, value_w, state_w, step_w, filt, misc, meta,
        resid_o, normed_o, pre_o, pre_halo_o, conv_o, vals_o, wr_o, shifted_o, cum_o, local_o, retain_o, pay_o,
        ext, state,
    ) = refs
    b = pl.program_id(0)
    span = GROUP
    lanes = value_w.shape[1]
    heads_rows = state.shape[0]

    def normalise(x):
        inv = lax.rsqrt(jnp.mean(x * x, axis=1, keepdims=True) + EPSILON)
        return (x * inv * gain[...]).astype(BFLOAT)

    @pl.when(b == 0)
    def _():
        rows = halo[...]
        if not first_layer:
            inv = lax.rsqrt(column(edge[EDGE : EDGE + 1, 512 - LANES : 512])[LANES - EDGE :] / INNER + EPSILON)
            rows = rows + inv * edge[0:EDGE]
        normed = normalise(rows)
        edge_pre = jnp.concatenate([nn(normed, value_w[...]), nn(normed, state_w[...])], axis=1)
        ext[0:EDGE] = edge_pre
        pre_halo_o[...] = edge_pre
        state[...] = jnp.zeros_like(state)

    @pl.when(b > 0)
    def _():
        ext[0:EDGE] = ext[span : span + EDGE]

    if first_layer:
        x = jnp.where(flags[1] == 1, tokens[...].astype(FLOAT), got[...])
    else:
        branch, inv_norm = branch_of(b, flags[2], mine, other)
        x = resid[...] + inv_norm * branch
    resid_o[...] = x
    normed = normalise(x)
    normed_o[...] = normed
    ext[EDGE : span + EDGE, 0:lanes] = nn(normed, value_w[...])
    ext[EDGE : span + EDGE, lanes:] = nn(normed, state_w[...])
    pre = ext[EDGE : span + EDGE]
    pre_o[...] = pre
    conv_sum = filt[CONV : CONV + 1] + filt[CONV - 1 : CONV] * pre
    for k in range(CONV - 1):
        at = EDGE - (CONV - 1) + k
        conv_sum = conv_sum + filt[k : k + 1] * (ext[at : at + span] * meta[:, k : k + 1])
    conv_o[...] = conv_sum
    activated = conv_sum * sigmoid(conv_sum)
    vals = activated[:, :lanes].astype(BFLOAT)
    write_read = activated[:, lanes:].astype(BFLOAT)
    vals_o[...] = vals
    wr_o[...] = write_read
    write = write_read[:, : write_read.shape[1] // 2]

    shifted = nt(normed, step_w[...]) + misc[2:3, 0:LANES]
    shifted_o[...] = shifted
    steps = softplus(shifted)
    log_decay = -misc[3:4, 0:LANES] * steps
    cum = nn(triangle(span, False), log_decay, PRECISE)
    cum_o[...] = cum
    last = cum[span - 1 : span]
    tail_step = meta[:, 4:5] * jnp.exp(last - cum) * steps
    heads = HEADS_OF(lanes)
    spread = spread_matrix(lanes, heads)
    weight = nn(tail_step, spread, PRECISE)
    local = tn((weight * vals.astype(FLOAT)).astype(BFLOAT), write)
    retain = meta[span - 1 : span, 3:4] * jnp.exp(last)
    retain_o[...] = jnp.broadcast_to(retain, retain_o.shape)
    size = heads_rows // heads
    local_o[...] = state[...]

    @pl.when(b == 0)
    def _():
        pay_o[heads_rows:] = jnp.ones_like(pay_o[heads_rows:])

    for h in range(heads):
        rows = slice(h * size, (h + 1) * size)
        state[rows] = retain[:, h : h + 1] * state[rows] + local[rows]
    pay_o[0:heads_rows] = state[...]
    pay_o[heads_rows:] = pay_o[heads_rows:] * retain


def HEADS_OF(lanes):
    return lanes // 64


def inside_kernel(normed, gate_w, vals, wr, cum, shifted, meta, seg_row, gate_o, y_o):
    lanes = vals.shape[1]
    heads = HEADS_OF(lanes)
    size = lanes // heads
    half = wr.shape[1] // 2
    gate_o[...] = nn(normed[...], gate_w[...])
    mask = within_block(meta[:, 5:6], seg_row[...])
    mixed = jnp.where(mask, nt(wr[:, half:], wr[:, :half]), 0.0)
    cum_v = cum[...]
    cum_t = cum_v.T
    step_t = softplus(shifted[...]).T
    for h in range(heads):
        gap = jnp.where(mask, cum_v[:, h : h + 1] - cum_t[h : h + 1, :], 0.0)
        mixing = (mixed * jnp.exp(gap) * step_t[h : h + 1, :]).astype(BFLOAT)
        y_o[:, h * size : (h + 1) * size] = nn(mixing, vals[:, h * size : (h + 1) * size])


def fold_in(me, count, payload, acc, reverse, heads):
    rows = acc.shape[0]
    size = rows // heads
    acc[...] = jnp.zeros_like(acc)
    for k in range(count):
        at = count - 1 - k if reverse else k
        reached = at > me if reverse else at < me

        @pl.when(reached)
        def _():
            keep = payload[at, rows : rows + 1]
            for h in range(heads):
                part = slice(h * size, (h + 1) * size)
                acc[part] = keep[:, h : h + 1] * acc[part] + payload[at, part]


def gated_kernel(
    flags, payload, local, retain, y, wr, vals, cum, meta, gate, misc, out_w, *rest, last_layer
):
    if last_layer:
        cot, got, ssm_o, states_o, partial_o, sums_o, cot_o, acc = rest
    else:
        ssm_o, states_o, partial_o, acc = rest
    b = pl.program_id(0)
    span, lanes = vals.shape
    heads = HEADS_OF(lanes)
    rows = acc.shape[0]
    size = rows // heads
    half = wr.shape[1] // 2

    @pl.when(b == 0)
    def _():
        fold_in(flags[0], payload.shape[0], payload, acc, False, heads)

    states = local[...] + acc[...]
    states_o[...] = states
    for h in range(heads):
        part = slice(h * size, (h + 1) * size)
        acc[part] = retain[0:1, h : h + 1] * acc[part]
    enter = meta[:, 3:4] * jnp.exp(cum[...])
    enter_lanes = nn(enter, spread_matrix(lanes, heads), PRECISE)
    carried = nt(wr[:, half:], states.astype(BFLOAT)) * enter_lanes
    ssm = y[...] + carried + misc[1:2] * vals[...].astype(FLOAT)
    ssm_o[...] = ssm
    gate_v = gate[...]
    gated = ssm * (gate_v * sigmoid(gate_v))
    partial = nn((gated * misc[0:1]).astype(BFLOAT), out_w[...])
    squares = nt(jnp.ones((8, lanes), FLOAT), gated * gated, PRECISE)
    if last_layer:
        partial_o[...] = partial
        sums_o[...] = jnp.zeros_like(sums_o)
        sums_o[0:1] = squares[0:1]
        given = jnp.where(flags[1] == 1, cot[...].astype(FLOAT), got[...])
        cot_o[...] = given
        sums_o[1:2] = nt(jnp.ones((8, partial.shape[1]), FLOAT), partial * given, PRECISE)[0:1]
    else:
        per = partial_o.shape[0] // 2
        inner = (per - EDGE) // span
        base = pl.multiple_of((b // inner) * per, EDGE)
        partial_o[pl.ds(pl.multiple_of(base + (b % inner) * span, EDGE), span)] = partial
        foot = pl.ds(pl.multiple_of(base + inner * span, EDGE), EDGE)

        @pl.when(b % inner == 0)
        def _():
            partial_o[foot] = jnp.zeros((EDGE, partial.shape[1]), FLOAT)

        for k in range(inner):

            @pl.when(b % inner == k)
            def _():
                partial_o[foot, k * span : (k + 1) * span] = squares


def ungate_kernel(flags, *refs, last_layer):
    if last_layer:
        (upstream, sums), refs = refs[:2], refs[2:]
    else:
        (cot, above_mine, above_other, above_x, above_gain, mine, other), refs = refs[:7], refs[7:]
    (normed, out_w, misc, gate, ssm, vals, wr, cum, meta, retain), refs = refs[:10], refs[10:]
    if not last_layer:
        (up_o, gain_o), refs = refs[:2], refs[2:]
    grad_ssm_o, gate_low_o, packed_o, small_o, later_o, pay_o, state, grad_gate_w_o, grad_out_w_o = refs
    b = pl.program_id(0)
    block = pl.num_programs(0) - 1 - b
    lanes = vals.shape[1]
    heads = HEADS_OF(lanes)
    rows = state.shape[0]
    size = rows // heads
    half = wr.shape[1] // 2

    @pl.when(b == 0)
    def _():
        state[...] = jnp.zeros_like(state)
        grad_out_w_o[...] = jnp.zeros_like(grad_out_w_o)
        grad_gate_w_o[...] = jnp.zeros_like(grad_gate_w_o)
        small_o[...] = jnp.zeros_like(small_o)
        pay_o[rows:] = jnp.ones_like(pay_o[rows:])
        if not last_layer:
            gain_o[...] = jnp.zeros_like(gain_o)

    if last_layer:
        up = upstream[...]
        sums_t = sums[...].T
        inv_norm = lax.rsqrt(sums_t[:, 0:1] / INNER + EPSILON)
        grad_inv = sums_t[:, 1:2]
    else:
        grad_normed, _, _ = summed(block, flags[2], above_mine, above_other)
        x = above_x[...]
        inv_rms = lax.rsqrt(jnp.mean(x * x, axis=1, keepdims=True) + EPSILON)
        scaled = x * inv_rms
        gain_o[0:1] += jnp.sum(grad_normed * scaled, axis=0, keepdims=True)
        inner = grad_normed * above_gain[...]
        up = cot[...] + inv_rms * (inner - scaled * jnp.mean(inner * scaled, axis=1, keepdims=True))
        up_o[...] = up
        branch, inv_norm = branch_of(block, flags[2], mine, other)
        grad_inv = jnp.sum(up * branch, axis=1, keepdims=True)

    grad_branch = (inv_norm * up).astype(BFLOAT)
    gate_v = gate[...]
    sigma = sigmoid(gate_v)
    gate_act = gate_v * sigma
    ssm_v = ssm[...]
    gated = ssm_v * gate_act
    gain = misc[0:1]
    out_in = (gated * gain).astype(BFLOAT)
    grad_out_w_o[...] += tn(out_in, grad_branch)
    grad_out_in = nt(grad_branch, out_w[...])
    small_o[0:1] += jnp.sum(grad_out_in * gated, axis=0, keepdims=True)
    grad_gated = grad_out_in * gain - (grad_inv * inv_norm * inv_norm * inv_norm / INNER) * gated
    grad_ssm = (grad_gated * gate_act).astype(BFLOAT)
    grad_ssm_o[...] = grad_ssm
    gate_low = (grad_gated * ssm_v * (sigma * (1.0 + gate_v * (1.0 - sigma)))).astype(BFLOAT)
    gate_low_o[...] = gate_low
    grad_gate_w_o[...] += tn(normed[...], gate_low)
    grad_wide = grad_ssm.astype(FLOAT)
    small_o[1:2] += jnp.sum(grad_wide * vals[...].astype(FLOAT), axis=0, keepdims=True)
    enter = meta[:, 3:4] * jnp.exp(cum[...])
    enter_lanes = nn(enter, spread_matrix(lanes, heads), PRECISE)
    pulls = tn((enter_lanes * grad_wide).astype(BFLOAT), wr[:, half:])
    later_o[...] = state[...]
    keep = retain[0:1]
    for h in range(heads):
        part = slice(h * size, (h + 1) * size)
        state[part] = keep[:, h : h + 1] * state[part] + pulls[part]
    pay_o[0:rows] = state[...]
    pay_o[rows:] = pay_o[rows:] * keep

    @pl.when(block == 0)
    def _():
        count = packed_o.shape[0]
        size = grad_gate_w_o.shape[0] // count
        half = size // 2
        for j in range(count):
            packed_o[j, 0:size] = grad_gate_w_o[j * size : (j + 1) * size]
            packed_o[j, size : size + half] = grad_out_w_o[j * half : (j + 1) * half, 0:lanes]
            packed_o[j, size + half :] = grad_out_w_o[j * half : (j + 1) * half, lanes:]


def unmix_kernel(
    flags, payload, later, retain, grad_ssm, vals, wr, cum, shifted, meta, seg_row, states, conv, pre, before, pre_halo,
    filt, misc,
    low_o, edge_o, step_low_o, spill_o, small_o, small2_o,
    acc, flows, ext,
):
    b = pl.program_id(0)
    blocks = pl.num_programs(0)
    span, lanes = vals.shape
    heads = HEADS_OF(lanes)
    rows = acc.shape[0]
    size = rows // heads
    half = wr.shape[1] // 2
    write, read = wr[:, :half], wr[:, half:]

    @pl.when(b == 0)
    def _():
        fold_in(flags[0], payload.shape[0], payload, acc, True, heads)
        small_o[...] = jnp.zeros_like(small_o)
        small2_o[...] = jnp.zeros_like(small2_o)
        for k in range(CONV - 1):
            ext[k, span:] = jnp.zeros_like(ext[k, span:])

    @pl.when(b > 0)
    def _():
        for k in range(CONV - 1):
            ext[k, span:] = ext[k, 0:EDGE]

    grad_next = later[...] + acc[...]
    keep = retain[0:1]
    states_v = states[...]
    spread = spread_matrix(lanes, heads)
    meet = jnp.sum(grad_next * states_v, axis=1, keepdims=True)
    grad_retain = tn(jnp.broadcast_to(meet, (rows, LANES)) * spread.T, jnp.ones((rows, 8), FLOAT), PRECISE)
    grad_retain = grad_retain.T[0:1]
    for h in range(heads):
        part = slice(h * size, (h + 1) * size)
        acc[part] = keep[:, h : h + 1] * acc[part]

    cum_v = cum[...]
    cum_t = cum_v.T
    shifted_v = shifted[...]
    steps = softplus(shifted_v)
    step_t = steps.T
    seg_mask = within_block(meta[:, 5:6], seg_row[...])
    inter = jnp.where(seg_mask, nt(read, write), 0.0)
    grad_inter = jnp.zeros((span, span), FLOAT)
    flows[...] = jnp.zeros_like(flows)
    parts = []
    row_sums = jnp.zeros((span, LANES), FLOAT)
    lane_no = lax.broadcasted_iota(jnp.int32, (span, LANES), 1)
    for h in range(heads):
        part = slice(h * size, (h + 1) * size)
        decay = jnp.exp(jnp.where(seg_mask, cum_v[:, h : h + 1] - cum_t[h : h + 1, :], 0.0))
        decay_inter = decay * inter
        step_h = step_t[h : h + 1, :]
        mixing = (decay_inter * step_h).astype(BFLOAT)
        grad_h = grad_ssm[:, part]
        parts.append(tn(mixing, grad_h))
        pairing = nt(grad_h, vals[:, part])
        grad_inter = grad_inter + pairing * decay * step_h
        weighted = pairing * decay_inter
        col = jnp.sum(weighted, axis=0, keepdims=True)
        flows[h : h + 1, :] = col
        row_sums = row_sums + jnp.where(
            lane_no == h, jnp.sum(weighted * step_h, axis=1, keepdims=True), 0.0
        )
    grad_vals = jnp.concatenate(parts, axis=1)
    grad_steps = flows[...].T
    grad_cum = row_sums - grad_steps * steps
    grad_inter = jnp.where(seg_mask, grad_inter, 0.0).astype(BFLOAT)
    grad_read = nn(grad_inter, write)
    grad_write = tn(grad_inter, read)

    vals_f = vals[...].astype(FLOAT)
    grad_f = grad_ssm[...].astype(FLOAT)
    enter = meta[:, 3:4] * jnp.exp(cum_v)
    enter_lanes = nn(enter, spread, PRECISE)
    states_low = states_v.astype(BFLOAT)
    grad_read = grad_read + nn((enter_lanes * grad_f).astype(BFLOAT), states_low)
    out_of = nt(read, states_low)
    grad_cum = grad_cum + enter * nt(grad_f * out_of, spread, PRECISE)
    next_low = grad_next.astype(BFLOAT)
    along = nt(write, next_low)
    last = cum_v[span - 1 : span]
    tail = meta[:, 4:5] * jnp.exp(last - cum_v)
    tail_step = tail * steps
    tail_lanes = nn(tail_step, spread, PRECISE)
    grad_vals = grad_vals + tail_lanes * along + misc[1:2] * grad_f
    grad_write = grad_write + nn((tail_lanes * vals_f).astype(BFLOAT), next_low)
    reach = nt(vals_f * along, spread, PRECISE)
    grad_steps = grad_steps + tail * reach
    tail_flow = tail_step * reach
    grad_last = jnp.sum(tail_flow, axis=0, keepdims=True) + grad_retain * keep
    grad_log = nn(triangle(span, True), grad_cum - tail_flow, PRECISE) + grad_last
    rate_v = misc[3:4, 0:LANES]
    log_decay = -rate_v * steps
    small2_o[0:1] += jnp.sum(grad_log * log_decay, axis=0, keepdims=True)
    grad_shifted = (grad_steps - rate_v * grad_log) * sigmoid(shifted_v)
    small2_o[1:2] += jnp.sum(grad_shifted, axis=0, keepdims=True)
    step_low_o[...] = grad_shifted.astype(BFLOAT)

    grad_conv = jnp.concatenate([grad_vals, grad_write, grad_read], axis=1) * silu_slope(conv[...])
    small_o[CONV : CONV + 1] += jnp.sum(grad_conv, axis=0, keepdims=True)
    pre_v = pre[...]
    small_o[CONV - 1 : CONV] += jnp.sum(grad_conv * pre_v, axis=0, keepdims=True)
    grad_pre = filt[CONV - 1 : CONV] * grad_conv
    first = blocks - 1 - b == 0
    for k in range(CONV - 1):
        lag = CONV - 1 - k
        masked = grad_conv * meta[:, k : k + 1]
        ext[k, 0:span] = masked
        ahead = ext[k, lag : lag + span]
        row_no = lax.broadcasted_iota(jnp.int32, (span, 1), 0)
        own = jnp.where(row_no < span - lag, ahead, 0.0)
        edge = jnp.where(first, pre_halo[...], before[...])
        head_rows = ext[k, 0:EDGE]
        edge_sum = jnp.zeros((1, head_rows.shape[1]), FLOAT)
        for t in range(lag):
            edge_sum = edge_sum + head_rows[t : t + 1] * edge[EDGE - lag + t : EDGE - lag + t + 1]
        small_o[k : k + 1] += jnp.sum(own * pre_v, axis=0, keepdims=True) + edge_sum
        grad_pre = grad_pre + filt[k : k + 1] * ahead
    low_o[...] = grad_pre.astype(BFLOAT)

    @pl.when(b == 0)
    def _():
        edge_o[...] = grad_pre[span - EDGE :]

    spill_o[...] = jnp.zeros_like(spill_o)
    for k in range(CONV - 1):
        lag = CONV - 1 - k
        for t in range(lag):
            at = EDGE - lag + t
            spill_o[at : at + 1] += filt[k : k + 1] * ext[k, t : t + 1]


def common_places(count, size):
    for j in range(count):
        for group in range(3):
            at = group * count * size + j * size
            side, row = divmod(at, 3 * count * size // 2)
            yield j, group, side, row


def weights_kernel(
    normed, low, edge, spill, gate_low, step_low, gate_w, value_w, state_w, step_w,
    small, small_c, small_h,
    grad_normed_o, packed_o,
    value_a, common_a, step_a,
):
    b = pl.program_id(0)
    blocks = pl.num_programs(0)
    span = low.shape[0]
    lanes = value_w.shape[1]
    d = value_w.shape[0]

    @pl.when(b == 0)
    def _():
        value_a[...] = jnp.zeros_like(value_a)
        common_a[...] = jnp.zeros_like(common_a)
        step_a[...] = jnp.zeros_like(step_a)

    patch = edge[...] + spill[...]
    padded = jnp.concatenate([jnp.zeros((span - EDGE, patch.shape[1]), FLOAT), patch], axis=0)
    row_no = lax.broadcasted_iota(jnp.int32, (span, 1), 0)
    use = (row_no >= span - EDGE) & (b == blocks - 1)
    low_v = jnp.where(use, padded, low[...].astype(FLOAT)).astype(BFLOAT)
    value_low, state_low = low_v[:, :lanes], low_v[:, lanes:]
    normed_v = normed[...]
    value_a[...] += tn(normed_v, value_low)
    common_a[0:d] += tn(normed_v, state_low)
    step_a[...] += tn(step_low[...], normed_v)
    grad_normed_o[...] = (
        nt(gate_low[...], gate_w[...])
        + nt(value_low, value_w[...])
        + nt(state_low, state_w[...])
        + nn(step_low[...], step_w[...])
    )

    @pl.when(b == blocks - 1)
    def _():
        common_a[d : d + EDGE] = small_c[0:EDGE, lanes:]
        count = packed_o.shape[0]
        size = d // count
        rows = size
        for j in range(count):
            packed_o[j, 0:size] = value_a[j * size : (j + 1) * size]
        packed_o[0, rows : rows + 5] = small_c[0:5, 0:lanes]
        packed_o[0, rows + 5 : rows + 7] = small[0:2]
        packed_o[0, rows + 7 : rows + 8, 0:LANES] = small_h[0:1]
        packed_o[0, rows + 7 : rows + 8, LANES : 2 * LANES] = small_h[1:2]
        packed_o[0, rows + 7 : rows + 8, 2 * LANES :] = jnp.zeros((1, lanes - 2 * LANES), FLOAT)
        packed_o[1, rows : rows + 8] = jnp.zeros((8, lanes), FLOAT)
        packed_o[2, rows : rows + 8] = step_a[0:8, 0:lanes]
        packed_o[3, rows : rows + 8] = step_a[0:8, lanes:]
        rows += 8
        part = packed_o.shape[1] - rows
        for j, group, side, row in common_places(count, part):
            packed_o[j, rows:, group * LANES : (group + 1) * LANES] = common_a[
                row : row + part, side * LANES : (side + 1) * LANES
            ]


AXES = ("dp", "ctx", "tensor")


def move(shard, dest):
    sizes = [lax.axis_size(axis) for axis in AXES]
    pairs = []
    for dp in range(sizes[0]):
        for q in range(sizes[1]):
            for t in range(sizes[2]):
                to = dest(dp, q, t)
                if to is not None:
                    pairs.append(
                        ((dp * sizes[1] + q) * sizes[2] + t, (to[0] * sizes[1] + to[1]) * sizes[2] + to[2])
                    )
    return lax.ppermute(shard, AXES, pairs)


def other_core(dp, q, t):
    return dp ^ 1, q, t


def beside(dp, q, t):
    return dp, q, t ^ 1


def at_home(dp, t):
    return t // 2 == dp % 2


class Where:
    def __init__(self):
        self.core = lax.axis_index("dp") % 2
        self.q = lax.axis_index("ctx")
        self.t = lax.axis_index("tensor")
        self.high = self.t // 2
        self.low = self.t % 2
        self.home = self.core == self.high
        self.count = lax.axis_size("ctx")
        self.flags = jnp.stack([self.q, self.home, self.core, self.t]).astype(jnp.int32)
        self.outer = lax.axis_size("dp") // 2


def piece(array, at, count):
    size = array.shape[0] // count
    return lax.dynamic_slice_in_dim(array, at * size, size)


def in_order(w, pieces):
    size = pieces[0].shape[0]
    full = jnp.zeros((size * len(pieces),) + pieces[0].shape[1:], pieces[0].dtype)
    for k, part in enumerate(pieces):
        full = lax.dynamic_update_slice_in_dim(full, part, (w.q ^ k) * size, 0)
    return full


def from_core(w, array):
    got = move(array, lambda dp, q, t: (dp ^ 1, q, t) if at_home(dp, t) else None)
    return jnp.where(w.home, array, got)


def tie(w, array, event):
    first = event[(0,) * event.ndim].astype(array.dtype)
    return array + jnp.where(w.q > 1000, first, jnp.zeros_like(first))


def pack_kernel(flags, value, gate, out, taps, off, gain, bias, decay, skip, step, *outs, layers):
    lanes = value.shape[2]
    d = value.shape[1]
    size = d // 4
    half = size // 2
    heads = step.shape[2]
    for l, parts in layers:
        places = [(outs[number], at) for number, at in parts]
        (first, base), (second, then) = places
        rows = pl.ds(pl.multiple_of(flags[0] * size, size), size)
        first[base : base + size] = value[l, rows].astype(FLOAT)
        base += size
        first[base : base + 16] = jnp.zeros((16, lanes), FLOAT)
        first[base : base + CONV] = taps[l]
        first[base + CONV : base + CONV + 1] = off[l : l + 1]
        first[base + CONV + 1 : base + CONV + 2] = gain[l : l + 1]
        first[base + 6 : base + 7, 0:heads] = bias[l : l + 1]
        first[base + 7 : base + 8, 0:heads] = decay[l : l + 1]
        first[base + 8 : base + 9, 0:heads] = skip[l : l + 1]
        wide = jnp.concatenate([step[l].astype(FLOAT), jnp.zeros((d, LANES - heads), FLOAT)], axis=1).T
        first[base + 16 : base + 24] = wide[0:8, 0:lanes]
        first[base + 24 : base + 32] = wide[0:8, lanes:]
        second[then : then + size] = gate[l, rows].astype(FLOAT)
        half_rows = pl.ds(pl.multiple_of(flags[0] * half, half), half)
        wide = out[l, half_rows].astype(FLOAT)
        second[then + size : then + size + half] = wide[:, 0:lanes]
        second[then + size + half : then + 2 * size] = wide[:, lanes:]


def value_kernel(flags, value, own, state_taps, state_off, *rest, layer):
    pieces, (value_o, step_o, filt_o, misc_o) = rest[:-4], rest[-4:]
    d, lanes = value_o.shape
    size = d // len(pieces)
    heads = HEADS_OF(lanes)

    @pl.when(flags[1] == 1)
    def _():
        value_o[...] = value[...]

    @pl.when(flags[1] == 0)
    def _():
        for k, part in enumerate(pieces):
            at = pl.multiple_of((flags[0] ^ k) * size, size)
            value_o[pl.ds(at, size)] = part[0:size].astype(BFLOAT)

    small = jnp.where(flags[1] == 1, own[size : size + 32], pieces[0][size : size + 32])
    step_o[...] = jnp.zeros_like(step_o)
    step_o[0:16, 0:lanes] = jnp.concatenate([small[16:24], jnp.zeros((8, lanes), FLOAT)]).astype(BFLOAT)
    step_o[0:16, lanes:] = jnp.concatenate([small[24:32], jnp.zeros((8, lanes), FLOAT)]).astype(BFLOAT)
    filt_o[...] = jnp.zeros_like(filt_o)
    filt_o[0 : CONV + 1, 0:lanes] = small[0 : CONV + 1]
    filt_o[0:CONV, lanes:] = state_taps[layer]
    filt_o[CONV : CONV + 1, lanes:] = state_off[layer : layer + 1]
    misc_o[...] = jnp.zeros_like(misc_o)
    misc_o[0:1] = small[CONV + 1 : CONV + 2]
    skip = jnp.broadcast_to(small[8:9, 0:LANES], (8, LANES))
    misc_o[1:2] = nn(skip, spread_matrix(lanes, heads), PRECISE)[0:1]
    misc_o[2:3, 0:LANES] = small[6:7, 0:LANES]
    lane_no = lax.broadcasted_iota(jnp.int32, (1, LANES), 1)
    misc_o[3:4, 0:LANES] = jnp.where(lane_no < heads, jnp.exp(small[7:8, 0:LANES]), 0.0)


def gate_kernel(flags, gate, out, *rest, base):
    pieces, (gate_o, out_o) = rest[:-2], rest[-2:]
    d, lanes = gate_o.shape
    size = d // len(pieces)
    half = size // 2

    @pl.when(flags[1] == 1)
    def _():
        gate_o[...] = gate[...]
        out_o[...] = out[...]

    @pl.when(flags[1] == 0)
    def _():
        for k, part in enumerate(pieces):
            at = pl.multiple_of((flags[0] ^ k) * size, size)
            gate_o[pl.ds(at, size)] = part[base : base + size].astype(BFLOAT)
            at = pl.multiple_of((flags[0] ^ k) * half, half)
            out_o[pl.ds(at, half), 0:lanes] = part[base + size : base + size + half].astype(BFLOAT)
            out_o[pl.ds(at, half), lanes:] = part[base + size + half : base + 2 * size].astype(BFLOAT)


def fetch_part(packed):
    return move(packed, lambda dp, q, t: (dp, q, t ^ 2) if at_home(dp, t) else None)


def fetch_rest(w, part):
    return [part] + [
        move(part, lambda dp, q, t, k=k: None if at_home(dp, t) else (dp, q ^ k, t)) for k in range(1, w.count)
    ]


def layer_spec(shape, layer):
    return pl.BlockSpec((None,) + tuple(shape[1:]), lambda b: (layer,) + (0,) * (len(shape) - 1))


def delivered_kernel(flags, own, got, *rest):
    gate_o, value_o, out_o, rows_o, state_o, extra_o, gain_o, wide = rest[-8:]
    count = own.shape[0]
    d, lanes = value_o.shape
    size = d // count
    half = size // 2
    rows = 3 * size
    part = own.shape[1] - rows - 16

    def put(source):
        total = jnp.zeros((8, lanes), FLOAT)
        for j in range(count):
            k = flags[0] ^ j
            gate_o[j * size : (j + 1) * size] = source[k, 0:size]
            out_o[j * half : (j + 1) * half, 0:lanes] = source[k, size : size + half]
            out_o[j * half : (j + 1) * half, lanes:] = source[k, size + half : 2 * size]
            value_o[j * size : (j + 1) * size] = source[k, 2 * size : rows]
            rows_o[j * 8 : (j + 1) * 8] = source[k, rows : rows + 8]
            total = total + source[k, rows + 8 + part :]
        for j, group, side, row in common_places(count, part):
            wide[row : row + part, side * LANES : (side + 1) * LANES] = source[
                flags[0] ^ j, rows + 8 : rows + 8 + part, group * LANES : (group + 1) * LANES
            ]
        gain_o[...] = total
        state_o[...] = wide[0:d]
        extra_o[...] = wide[d : d + 8]

    @pl.when(flags[1] == 1)
    def _():
        put(own)

    @pl.when(flags[1] == 0)
    def _():
        put(got)


def joined_kernel(flags, have, got, out):
    own = pl.program_id(0) == flags[2]

    @pl.when(own)
    def _():
        out[...] = have[...].astype(BFLOAT)

    @pl.when(jnp.logical_not(own))
    def _():
        out[...] = got[...].astype(BFLOAT)


def halves(w, array):
    return piece(array, w.core, 2) + move(piece(array, 1 - w.core, 2), other_core)


def add_up(w, array, tied=None):
    first = halves(w, array)
    got = move(first, beside)
    part = first + (tied(first, got) if tied else got)
    return first, part, move(part, other_core)


def add_small(array):
    array = array + move(array, other_core)
    return array + move(array, beside)


def add_rows(w, array):
    part = halves(w, array)
    return piece(part, w.low, 2) + move(piece(part, 1 - w.low, 2), beside)


def hand_step(w, up, down):
    count = lax.axis_size("tensor")
    return (
        move(up, lambda dp, q, t: (dp, q, t + 1) if t + 1 < count else None),
        move(down, lambda dp, q, t: (dp, q, t - 1) if t > 0 else None),
    )


def hand_out(w, rows):
    up, down, steps = rows, rows, []
    for _ in range(lax.axis_size("tensor") - 1):
        up, down = hand_step(w, up, down)
        steps.append((up, down))
        up, down = tie(w, up, down), tie(w, down, up)
    return steps


def hand_out_end(w, rows, steps):
    def unit(j):
        total = jnp.where(w.t == j, rows, 0.0)
        for k, (up, down) in enumerate(steps, 1):
            total = jnp.where(w.t == j + k, up, jnp.where(w.t == j - k, down, total))
        return total

    units = [unit(j) for j in range(len(steps) + 1)]
    low, high = jnp.concatenate(units[:2]), jnp.concatenate(units[2:])
    have = jnp.where(w.core == 0, low, high)
    got = move(jnp.where(w.core == 0, high, low), other_core)
    (out,) = call(
        joined_kernel, 2,
        [(w.flags, "smem"), (have, "whole"), (got, "whole")],
        [((2 * have.shape[0], have.shape[1]), BFLOAT, "rows")],
    )
    return out


def over_outer(w, part):
    total = part
    for k in range(1, w.outer):
        size = 2 * w.outer
        total = total + move(part, lambda dp, q, t, k=k: ((dp + 2 * k) % size, q, t))
    return total


def total_start(w, packed, event):
    def at(k):
        return tie(w, lax.dynamic_index_in_dim(packed, w.q ^ k, 0, keepdims=False), event)

    return [at(0)] + [move(at(k), lambda dp, q, t, k=k: (dp, q ^ k, t)) for k in range(1, w.count)]


def total_middle(w, part_a, got, shard_rows, gains, event):
    part = over_outer(w, tie(w, sum(got[1:], got[0]), event))

    def across(array):
        return move(array, lambda dp, q, t: None if at_home(dp, t) else (dp, q, t ^ 2))

    main = jnp.concatenate([part_a, part[:shard_rows]])
    main_far = across(main)
    common = jnp.concatenate([part[shard_rows:], gains])
    common = common + move(common, other_core)
    common = common + move(common, beside)
    return jnp.concatenate([main, common]), jnp.concatenate([main_far, across(common)])


def total_spread(w, part, far, event):
    part = tie(w, part + far, event)
    got = [
        move(part, lambda dp, q, t, k=k: (dp, q ^ k, t) if at_home(dp, t) else None) for k in range(1, w.count)
    ]
    return part, got


def total_end(w, layer, part, got, shapes, before):
    own = jnp.stack([part] + got)
    got = move(own, lambda dp, q, t: (dp ^ 1, q, t) if at_home(dp, t) else None)
    inputs = [(w.flags, "smem"), (own, "whole"), (got, "whole")]
    aliases = {}
    if before is not None:
        aliases = {len(inputs) + i: i for i in range(len(before))}
        inputs += [(array, pl.BlockSpec(memory_space=pl.ANY)) for array in before]
    d, half = shapes[0][1], shapes[4][2]
    return call(
        delivered_kernel, 1, inputs, [(shape, FLOAT, layer_spec(shape, layer)) for shape in shapes],
        [pltpu.VMEM((6 * (own.shape[1] - 3 * d // 4 - 16), half), FLOAT)], aliases=aliases,
    )


def passed_along(shard, axis, by):
    count = lax.axis_size(axis)
    pairs = [(i, i + by) for i in range(count) if 0 <= i + by < count]
    return lax.ppermute(shard, axis, pairs)


def forward_layer(w, source, wts, geometry, given=None, deps=(), then=lambda event: ()):
    meta, seg_row = geometry
    first = len(source) == 3
    n, d = source[0].shape
    grid = n // GROUP
    lanes = wts["value_w"].shape[1]
    wide = wts["state_w"].shape[1]
    chans = lanes + wide
    state = wide // 2
    pay = (lanes + 8, state)
    if first:
        got = pl.BlockSpec((GROUP, d), lambda b: (b, 0))
        entry = [(source[0], "rows"), (source[1], got), (source[2], "whole")]
    else:
        entry = [(source[0], "rows")] + [(array, "whole") for array in source[1:]]
    x, normed, pre, pre_halo, conv, vals, wr, shifted, cum, local, retain, payload = call(
        functools.partial(project_kernel, first_layer=first), grid,
        [(w.flags, "smem")] + entry + [
            (wts["gain"], "whole"), (wts["value_w"], "whole"), (wts["state_w"], "whole"), (wts["step_w"], "whole"),
            (wts["filt"], "whole"), (wts["misc"], "whole"), (meta, "rows"),
        ],
        [
            ((n, d), FLOAT, "rows"), ((n, d), BFLOAT, "rows"), ((n, chans), FLOAT, "rows"),
            ((EDGE, chans), FLOAT, "whole"), ((n, chans), FLOAT, "rows"), ((n, lanes), BFLOAT, "rows"),
            ((n, wide), BFLOAT, "rows"), ((n, LANES), FLOAT, "rows"), ((n, LANES), FLOAT, "rows"),
            ((grid, lanes, state), FLOAT, "lead"), ((grid, 8, LANES), FLOAT, "lead"), (pay, FLOAT, "whole"),
        ],
        [pltpu.VMEM((GROUP + EDGE, chans), FLOAT), pltpu.VMEM((lanes, state), FLOAT)],
        flops=2 * n * d * chans,
        deps=deps,
    )
    everything = lax.all_gather(payload, "ctx")
    gate_w, out_w = wts["late"](payload)
    gate, y = call(
        inside_kernel, grid,
        [(normed, "rows"), (gate_w, "whole"), (vals, "rows"), (wr, "rows"), (cum, "rows"),
         (shifted, "rows"), (meta, "rows"), (seg_row, "lead")],
        [((n, lanes), FLOAT, "rows"), ((n, lanes), FLOAT, "rows")],
        flops=4 * n * GROUP * lanes,
        deps=then(payload),
    )
    last = given is not None
    extra = [(given[0], "rows"), (given[1], "rows")] if last else []
    if last:
        results = [((n, d), FLOAT, "rows"), ((grid, 8, GROUP), FLOAT, "lead"), ((n, d), FLOAT, "rows")]
    else:
        results = [((n + 2 * EDGE, d), FLOAT, "whole")]
    outs = call(
        functools.partial(gated_kernel, last_layer=last), grid,
        [
            (w.flags, "smem"), (everything, "whole"), (local, "lead"), (retain, "lead"), (y, "rows"), (wr, "rows"),
            (vals, "rows"), (cum, "rows"), (meta, "rows"), (gate, "rows"), (wts["misc"], "whole"), (out_w, "whole"),
        ] + extra,
        [((n, lanes), FLOAT, "rows"), ((grid, lanes, state), FLOAT, "lead")] + results,
        [pltpu.VMEM((lanes, state), FLOAT)],
        flops=2 * n * d * lanes,
    )
    ssm, states = outs[0], outs[1]
    saved = (normed, gate, pre, pre_halo, conv, vals, wr, shifted, cum, retain, ssm, states, gate_w, out_w)
    return x, outs[2:], saved


def backward_layer(w, source, wts, saved, geometry, deps):
    meta, seg_row = geometry
    normed, gate, pre, pre_halo, conv, vals, wr, shifted, cum, retain, ssm, states, gate_w, out_w = saved
    last = len(source) == 2
    n, d = source[0].shape
    grid = n // GROUP
    lanes = vals.shape[1]
    chans = pre.shape[1]
    state = wr.shape[1] // 2
    pay = (lanes + 8, state)
    if last:
        entry = [(source[0], "rows"), (source[1], "lead")]
        above = []
    else:
        kinds = ["rows", "whole", "whole", "rows", "whole", "whole", "whole"]
        entry = list(zip(source, kinds))
        above = [((n, d), FLOAT, "rows"), ((8, d), FLOAT, "whole")]
    outs = call(
        functools.partial(ungate_kernel, last_layer=last), grid,
        [(w.flags, "smem")] + entry + [
            (normed, "rows"), (out_w, "whole"), (wts["misc"], "whole"), (gate, "rows"), (ssm, "rows"),
            (vals, "rows"), (wr, "rows"), (cum, "rows"), (meta, "rows"), (retain, "lead"),
        ],
        above + [
            ((n, lanes), BFLOAT, "rows"), ((n, lanes), BFLOAT, "rows"), ((4, d // 2, lanes), FLOAT, "whole"),
            ((8, lanes), FLOAT, "whole"), ((grid, lanes, state), FLOAT, "lead"), (pay, FLOAT, "whole"),
        ],
        [pltpu.VMEM((lanes, state), FLOAT), pltpu.VMEM((d, lanes), FLOAT), pltpu.VMEM((lanes, d), FLOAT)],
        reverse=True,
        flops=6 * n * d * lanes,
        deps=deps[0],
    )
    above = outs[: len(above)]
    grad_ssm, gate_low, packed_a, small, later, payload = outs[len(above) :]
    everything = lax.all_gather(payload, "ctx")
    got_a = total_start(w, packed_a, everything)
    strip = GROUP // EDGE
    before = pl.BlockSpec((EDGE, chans), lambda b: (jnp.maximum((grid - 1 - b) * strip - 1, 0), 0))
    low, edge, step_low, spill, small_c, small_h = call(
        unmix_kernel, grid,
        [
            (w.flags, "smem"), (everything, "whole"), (later, "lead"), (retain, "lead"), (grad_ssm, "rows"),
            (vals, "rows"), (wr, "rows"), (cum, "rows"), (shifted, "rows"), (meta, "rows"), (seg_row, "lead"),
            (states, "lead"), (conv, "rows"), (pre, "rows"), (pre, before), (pre_halo, "whole"),
            (wts["filt"], "whole"), (wts["misc"], "whole"),
        ],
        [
            ((n, chans), BFLOAT, "rows"), ((EDGE, chans), FLOAT, "whole"), ((n, LANES), BFLOAT, "rows"),
            ((EDGE, chans), FLOAT, "whole"), ((8, chans), FLOAT, "whole"), ((8, LANES), FLOAT, "whole"),
        ],
        [
            pltpu.VMEM((lanes, state), FLOAT), pltpu.VMEM((LANES, GROUP), FLOAT),
            pltpu.VMEM((CONV - 1, GROUP + EDGE, chans), FLOAT),
        ],
        reverse=True,
        flops=12 * n * GROUP * lanes,
        deps=deps[1](payload),
    )
    spill = passed_along(spill, "ctx", -1)
    part_a = over_outer(w, sum(got_a[1:], got_a[0]))
    common = 144
    grad_normed, packed = call(
        weights_kernel, grid,
        [
            (normed, "rows"), (low, "rows"), (edge, "whole"), (spill, "whole"), (gate_low, "rows"),
            (step_low, "rows"), (gate_w, "whole"), (wts["value_w"], "whole"), (wts["state_w"], "whole"),
            (wts["step_w"], "whole"), (small, "whole"),
            (small_c, "whole"), (small_h, "whole"),
        ],
        [((n, d), FLOAT, "rows"), ((4, d // 4 + 8 + common, lanes), FLOAT, "whole")],
        [pltpu.VMEM((d, lanes), FLOAT), pltpu.VMEM((6 * common, chans - lanes), FLOAT), pltpu.VMEM((LANES, d), FLOAT)],
        flops=4 * n * d * (lanes + chans),
        deps=deps[2](low) + [part_a],
    )
    return grad_normed, (part_a, packed), above


def local(tokens, segments, *rest):
    params, cotangent = rest[:-1], rest[-1]
    (
        in_gain, gate_w, value_w, state_w, step_w, value_filt, value_off, state_filt, state_off,
        bias_step, decay_param, skip_param, gain_out, out_w,
    ) = params
    n, d = tokens.shape
    w = Where()
    heads = step_w.shape[2]
    lanes = value_w.shape[2]
    wide = state_w.shape[2]
    size = d // w.count

    def pack(layers, shapes, deps=()):
        return call(
            functools.partial(pack_kernel, layers=layers), 1,
            [(w.flags, "smem")] + [
                (array, "whole") for array in (
                    value_w, gate_w, out_w, value_filt, value_off, gain_out, bias_step, decay_param, skip_param, step_w
                )
            ],
            [(shape, FLOAT, "whole") for shape in shapes],
            deps=deps,
        )

    def early(l, own, pieces):
        value, step, filt, misc = call(
            functools.partial(value_kernel, layer=l), 1,
            [(w.flags, "smem"), (value_w, layer_spec(value_w.shape, l)), (own, "whole"), (state_filt, "whole"),
             (state_off, "whole")] + [(part, "whole") for part in pieces],
            [((d, lanes), BFLOAT, "whole"), ((LANES, d), BFLOAT, "whole"), ((8, lanes + wide), FLOAT, "whole"),
             ((8, lanes), FLOAT, "whole")],
        )
        return dict(gain=in_gain[l][None], value_w=value, step_w=step, state_w=state_w[l], filt=filt, misc=misc)

    def late(l, pieces, base, deps=()):
        return call(
            functools.partial(gate_kernel, base=base), 1,
            [(w.flags, "smem"), (gate_w, layer_spec(gate_w.shape, l)), (out_w, layer_spec(out_w.shape, l))]
            + [(part, "whole") for part in pieces],
            [((d, lanes), BFLOAT, "whole"), ((lanes, d), BFLOAT, "whole")],
            deps=deps,
        )

    near = (size + 32, lanes)
    far = (2 * size, lanes)
    both = (near[0] + far[0], lanes)
    pack_a, pack_b, pack_1 = pack(((0, ((0, 0), (1, 0))), (1, ((2, 0), (2, near[0])))), (near, far, both))
    part_a = fetch_part(pack_a)
    edge = jnp.concatenate([
        tokens[n - EDGE :].astype(FLOAT),
        jnp.pad(segments[n - EDGE :].astype(FLOAT)[None], ((0, EDGE - 1), (0, d - EDGE))),
    ])
    edge = passed_along(edge, "ctx", 1)
    segs = jnp.pad(segments.astype(FLOAT), (0, 8 * d - n)).reshape(8, d)
    body = jnp.concatenate([tokens.astype(FLOAT), segs])
    body = move(body, lambda dp, q, t: (dp ^ 1, q, t) if at_home(dp, t) else None)
    part_b = fetch_part(tie(w, pack_b, part_a))
    edge = from_core(w, edge)
    segs = jnp.where(w.home, segs, body[n:]).reshape(-1)[:n]
    seg_ext = jnp.concatenate([edge[EDGE, :EDGE], segs])
    seg_blocks = segs.reshape(-1, GROUP)
    seg_before = jnp.concatenate([seg_ext[EDGE - 1 : EDGE], seg_blocks[:-1, -1]])
    first = EDGE - (CONV - 1)
    columns = [seg_ext[first + k : first + k + n] == segs for k in range(CONV - 1)]
    columns.append((seg_blocks == seg_before[:, None]).reshape(n))
    columns.append((seg_blocks == seg_blocks[:, -1:]).reshape(n))
    columns.append(segs)
    columns += [jnp.zeros_like(segs)] * (8 - len(columns))
    meta = jnp.stack([column.astype(FLOAT) for column in columns], axis=1)
    geometry = (meta, segs.reshape(-1, 1, GROUP))

    wts = [early(0, pack_a, fetch_rest(w, part_a))]
    wts[0]["late"] = lambda event: late(0, fetch_rest(w, part_b), 0, [event])
    halo = edge[:EDGE]
    sent = {"pack": pack_1}

    def send_next(event):
        sent["part"] = fetch_part(tie(w, sent["pack"], part_b))
        return [sent["part"]]

    x_0, (partial,), saved_0 = forward_layer(
        w, (tokens, body, halo), wts[0], geometry, deps=[part_b], then=send_next
    )

    def meanwhile(first, got):
        pieces = fetch_rest(w, tie(w, sent["part"], first))
        wts.append(early(1, sent["pack"], pieces))
        wts[1]["late"] = lambda event: late(1, pieces, near[0])
        sent["cot"] = move(
            tie(w, cotangent.astype(FLOAT), first),
            lambda dp, q, t: (dp ^ 1, q, t) if at_home(dp, t) else None,
        )
        return tie(w, got, wts[1]["misc"])

    _, mine, other = add_up(w, partial, meanwhile)
    edge_1 = mine[mine.shape[0] - 2 * EDGE :]
    from_last = [
        move(edge_1, lambda dp, q, t, c=c: (dp - 1 + c, q + 1, t) if dp % 2 == 1 and q + 1 < w.count else None)
        for c in (0, 1)
    ]
    edge_1 = from_last[0] + from_last[1]

    x_1, (partial, sums, cot), saved_1 = forward_layer(
        w, (x_0, mine, other, halo, edge_1), wts[1], geometry, (cotangent, sent["cot"])
    )
    sums = add_small(sums)
    quarter = 2 * w.core + w.low
    half = halves(w, partial)
    branch = piece(half, w.low, 2) + move(tie(w, piece(half, 1 - w.low, 2), sums), beside)
    rows_sq = lax.dynamic_index_in_dim(sums, quarter, 0, keepdims=False)[0]
    mixed = piece(x_1, quarter, 4) + lax.rsqrt(rows_sq / INNER + EPSILON)[:, None] * branch
    mixed_first = hand_step(w, mixed, mixed)

    grad_normed, packed, _ = backward_layer(
        w, (cot, sums), wts[1], saved_1, geometry,
        ([half], lambda event: [mixed], lambda event: list(mixed_first)),
    )
    held = {}

    def gather(first, got):
        held["start"] = total_start(w, packed[1], first)
        held["start"] = sum(held["start"][1:], held["start"][0])
        return tie(w, got, held["start"])

    _, above_mine, above_other = add_up(w, grad_normed, gather)
    part_1 = packed[0]
    shard_rows = size + 8
    none = jnp.zeros((8, lanes), FLOAT)

    up, down = (tie(w, array, above_mine) for array in mixed_first)
    mixed_second = hand_step(w, up, down)
    mixed_third = hand_step(w, tie(w, mixed_second[0], mixed_second[1]), tie(w, mixed_second[1], mixed_second[0]))
    mixed_steps = [mixed_first, mixed_second, mixed_third]

    def middle(event):
        held["part"], held["far"] = total_middle(w, part_1, [held["start"]], shard_rows, none, event)
        return [held["part"]] + list(mixed_second)

    def spread(event):
        held["part"], held["got"] = total_spread(w, held["part"], held["far"], event)
        return [held["part"]] + list(mixed_third)

    grad_normed, packed, (upstream, gain_1) = backward_layer(
        w, (cot, above_mine, above_other, x_1, in_gain[1][None], mine, other), wts[0], saved_0, geometry,
        ((), middle, spread),
    )
    shapes = (
        (LAYERS, d, lanes), (LAYERS, d, lanes), (LAYERS, lanes, d), (LAYERS, 32, lanes), (LAYERS, d, wide),
        (LAYERS, 8, wide), (LAYERS, 8, lanes),
    )
    first_half = halves(w, grad_normed)
    got = total_start(w, packed[1], first_half)
    last_part = piece(first_half, w.low, 2) + move(piece(first_half, 1 - w.low, 2), beside)
    x = piece(x_0, quarter, 4)
    inv_rms = lax.rsqrt(jnp.mean(x * x, axis=1, keepdims=True) + EPSILON)
    scaled = x * inv_rms
    gain_0 = jnp.sum(last_part * scaled, axis=0)
    inner = last_part * in_gain[0]
    last = piece(upstream, quarter, 4) + inv_rms * (
        inner - scaled * jnp.mean(inner * scaled, axis=1, keepdims=True)
    )
    steps = hand_out(w, last)
    totals = total_end(w, 1, tie(w, held["part"], steps[0][0]), held["got"], shapes, None)
    held["mixed"] = hand_out_end(w, mixed, mixed_steps[:2] + [(tie(w, mixed_third[0], last), mixed_third[1])])
    gains = jnp.concatenate([gain_0.reshape(-1, lanes), 0.25 * gain_1[0].reshape(-1, lanes)])
    gains = jnp.pad(gains, ((0, 8 - gains.shape[0]), (0, 0)))
    part, far = total_middle(w, packed[0], got, shard_rows, gains, steps[0][0])
    part, got = total_spread(w, part, far, steps[1][0])
    input_grad = hand_out_end(w, last, steps)
    grad_gate, grad_value, grad_out, rows, state, extra, gains = total_end(w, 0, part, got, shapes, totals)
    step = jnp.concatenate([rows[:, 16:24], rows[:, 24:32]], axis=2)
    step = jnp.swapaxes(step[:, :heads], 1, 2)
    return (
        held["mixed"], input_grad, gains[0, :4].reshape(2, d), grad_gate, grad_value, state, step, rows[:, :CONV],
        rows[:, CONV], extra[:, :CONV], extra[:, CONV], rows[:, 7, LANES : LANES + heads], rows[:, 7, :heads],
        jnp.sum(rows[:, 6].reshape(LAYERS, heads, -1), axis=2), rows[:, 5], grad_out,
    )


def solution(mesh):
    split = P(None, None, "tensor")
    lane = P(None, "tensor")
    rows = P(("dp", "ctx"), None)
    weights = (P(), split, split, P(), split, split, lane, P(), P(), lane, lane, lane, lane, P(None, "tensor", None))
    return jax.shard_map(
        local,
        mesh=mesh,
        in_specs=(rows, P(("dp", "ctx")), *weights, rows),
        out_specs=(rows, rows, *weights),
        check_vma=False,
    )
```

```python
import functools

import jax
import jax.numpy as jnp
from jax import lax
from jax.experimental import pallas as pl
from jax.experimental.pallas import tpu as pltpu
from jax.sharding import PartitionSpec as P

CONV = 4
GROUP = 256
LAYERS = 2
INNER = 1536
EDGE = 8
LANES = 128


EPSILON = 1e-05
PRECISE = lax.Precision.HIGHEST
FLOAT = jnp.float32
BFLOAT = jnp.bfloat16
VMEM_BYTES = 56 * 1024 * 1024


def nn(left, right, precision=None):
    return lax.dot_general(
        left, right, (((1,), (0,)), ((), ())), precision=precision, preferred_element_type=FLOAT
    )


def nt(left, right, precision=None):
    return lax.dot_general(
        left, right, (((1,), (1,)), ((), ())), precision=precision, preferred_element_type=FLOAT
    )


def tn(left, right, precision=None):
    return lax.dot_general(
        left, right, (((0,), (0,)), ((), ())), precision=precision, preferred_element_type=FLOAT
    )


def sigmoid(value):
    return 1.0 / (1.0 + jnp.exp(-value))


def softplus(value):
    small = jnp.exp(-jnp.abs(value))
    series = small * (1.0 - small * (0.5 - small * (1.0 / 3.0 - small * 0.25)))
    return jnp.maximum(value, 0.0) + jnp.where(small < 0.01, series, jnp.log(1.0 + small))


def silu_slope(value):
    sigma = sigmoid(value)
    return sigma * (1.0 + value * (1.0 - sigma))


def spread_matrix(lane_count, heads):
    size = lane_count // heads
    head = lax.broadcasted_iota(jnp.int32, (LANES, lane_count), 0)
    lane = lax.broadcasted_iota(jnp.int32, (LANES, lane_count), 1)
    return jnp.where((lane >= head * size) & (lane < (head + 1) * size), 1.0, 0.0).astype(FLOAT)


def triangle(span, upper):
    row = lax.broadcasted_iota(jnp.int32, (span, span), 0)
    col = lax.broadcasted_iota(jnp.int32, (span, span), 1)
    return jnp.where(col >= row if upper else col <= row, 1.0, 0.0).astype(FLOAT)


def within_block(seg_col, seg_row):
    span = seg_col.shape[0]
    row = lax.broadcasted_iota(jnp.int32, (span, span), 0)
    col = lax.broadcasted_iota(jnp.int32, (span, span), 1)
    return (row >= col) & (seg_col == seg_row)


def call(body, grid, inputs, outputs, scratch=(), reverse=False, flops=0, aliases=None, deps=()):
    def place(b):
        return grid - 1 - b if reverse else b

    def spec_of(shape, kind):
        if isinstance(kind, pl.BlockSpec):
            return kind
        if kind == "smem":
            return pl.BlockSpec(memory_space=pltpu.SMEM)
        if kind == "rows":
            return pl.BlockSpec((shape[0] // grid, shape[1]), lambda b: (place(b), 0))
        if kind == "lead":
            return pl.BlockSpec((None,) + tuple(shape[1:]), lambda b: (place(b),) + (0,) * (len(shape) - 1))
        return pl.BlockSpec(tuple(shape), lambda b: (0,) * len(shape))

    known = len(inputs)
    inputs = list(inputs) + [(dep, pl.BlockSpec(memory_space=pl.ANY)) for dep in deps]

    def run(*refs):
        body(*refs[:known], *refs[len(inputs) :])

    moved = sum(a.size * a.dtype.itemsize for a, _ in inputs)
    return pl.pallas_call(
        run,
        grid=(grid,),
        in_specs=[spec_of(a.shape, kind) for a, kind in inputs],
        out_specs=[spec_of(shape, kind) for shape, _, kind in outputs],
        out_shape=[jax.ShapeDtypeStruct(shape, dtype) for shape, dtype, _ in outputs],
        scratch_shapes=list(scratch),
        input_output_aliases=aliases or {},
        compiler_params=pltpu.CompilerParams(
            dimension_semantics=("arbitrary",), vmem_limit_bytes=VMEM_BYTES
        ),
        cost_estimate=pl.CostEstimate(flops=int(flops), bytes_accessed=int(2 * moved), transcendentals=0),
    )(*[a for a, _ in inputs])


def column(row):
    return jnp.broadcast_to(row, (8, row.shape[1])).T[:, 0:1]


def summed(b, core, mine, other):
    span = GROUP
    per = mine.shape[0] // span
    use = b // per == core
    rows = pl.ds(pl.multiple_of((b % per) * span, span), span)
    return jnp.where(use, mine[rows], other[rows]), use, b % per


def branch_of(b, core, mine, other):
    total, use, at = summed(b, core, mine, other)
    size = mine.shape[0] - EDGE
    squares = jnp.where(use, mine[size : size + 1], other[size : size + 1])
    row = squares[:, 0:GROUP]
    for k in range(1, size // GROUP):
        row = jnp.where(at == k, squares[:, k * GROUP : (k + 1) * GROUP], row)
    return total, lax.rsqrt(column(row) / INNER + EPSILON)


def project_kernel(flags, *refs, first_layer):
    if first_layer:
        (tokens, got, halo), refs = refs[:3], refs[3:]
    else:
        (resid, mine, other, halo, edge), refs = refs[:5], refs[5:]
    (
        gain, value_w, state_w, step_w, filt, misc, meta,
        resid_o, normed_o, pre_o, pre_halo_o, conv_o, vals_o, wr_o, shifted_o, cum_o, local_o, retain_o, pay_o,
        ext, state,
    ) = refs
    b = pl.program_id(0)
    span = GROUP
    lanes = value_w.shape[1]
    heads_rows = state.shape[0]

    def normalise(x):
        inv = lax.rsqrt(jnp.mean(x * x, axis=1, keepdims=True) + EPSILON)
        return (x * inv * gain[...]).astype(BFLOAT)

    @pl.when(b == 0)
    def _():
        rows = halo[...]
        if not first_layer:
            inv = lax.rsqrt(column(edge[EDGE : EDGE + 1, 512 - LANES : 512])[LANES - EDGE :] / INNER + EPSILON)
            rows = rows + inv * edge[0:EDGE]
        normed = normalise(rows)
        edge_pre = jnp.concatenate([nn(normed, value_w[...]), nn(normed, state_w[...])], axis=1)
        ext[0:EDGE] = edge_pre
        pre_halo_o[...] = edge_pre
        state[...] = jnp.zeros_like(state)

    @pl.when(b > 0)
    def _():
        ext[0:EDGE] = ext[span : span + EDGE]

    if first_layer:
        x = jnp.where(flags[1] == 1, tokens[...].astype(FLOAT), got[...])
    else:
        branch, inv_norm = branch_of(b, flags[2], mine, other)
        x = resid[...] + inv_norm * branch
    resid_o[...] = x
    normed = normalise(x)
    normed_o[...] = normed
    ext[EDGE : span + EDGE, 0:lanes] = nn(normed, value_w[...])
    ext[EDGE : span + EDGE, lanes:] = nn(normed, state_w[...])
    pre = ext[EDGE : span + EDGE]
    pre_o[...] = pre
    conv_sum = filt[CONV : CONV + 1] + filt[CONV - 1 : CONV] * pre
    for k in range(CONV - 1):
        at = EDGE - (CONV - 1) + k
        conv_sum = conv_sum + filt[k : k + 1] * (ext[at : at + span] * meta[:, k : k + 1])
    conv_o[...] = conv_sum
    activated = conv_sum * sigmoid(conv_sum)
    vals = activated[:, :lanes].astype(BFLOAT)
    write_read = activated[:, lanes:].astype(BFLOAT)
    vals_o[...] = vals
    wr_o[...] = write_read
    write = write_read[:, : write_read.shape[1] // 2]

    shifted = nt(normed, step_w[...]) + misc[2:3, 0:LANES]
    shifted_o[...] = shifted
    steps = softplus(shifted)
    log_decay = -misc[3:4, 0:LANES] * steps
    cum = nn(triangle(span, False), log_decay, PRECISE)
    cum_o[...] = cum
    last = cum[span - 1 : span]
    tail_step = meta[:, 4:5] * jnp.exp(last - cum) * steps
    heads = HEADS_OF(lanes)
    spread = spread_matrix(lanes, heads)
    weight = nn(tail_step, spread, PRECISE)
    local = tn((weight * vals.astype(FLOAT)).astype(BFLOAT), write)
    retain = meta[span - 1 : span, 3:4] * jnp.exp(last)
    retain_o[...] = jnp.broadcast_to(retain, retain_o.shape)
    size = heads_rows // heads
    local_o[...] = state[...]

    @pl.when(b == 0)
    def _():
        pay_o[heads_rows:] = jnp.ones_like(pay_o[heads_rows:])

    for h in range(heads):
        rows = slice(h * size, (h + 1) * size)
        state[rows] = retain[:, h : h + 1] * state[rows] + local[rows]
    pay_o[0:heads_rows] = state[...]
    pay_o[heads_rows:] = pay_o[heads_rows:] * retain


def HEADS_OF(lanes):
    return lanes // 64


def inside_kernel(normed, gate_w, vals, wr, cum, shifted, meta, seg_row, gate_o, y_o):
    lanes = vals.shape[1]
    heads = HEADS_OF(lanes)
    size = lanes // heads
    half = wr.shape[1] // 2
    gate_o[...] = nn(normed[...], gate_w[...])
    mask = within_block(meta[:, 5:6], seg_row[...])
    mixed = jnp.where(mask, nt(wr[:, half:], wr[:, :half]), 0.0)
    cum_v = cum[...]
    cum_t = cum_v.T
    step_t = softplus(shifted[...]).T
    for h in range(heads):
        gap = jnp.where(mask, cum_v[:, h : h + 1] - cum_t[h : h + 1, :], 0.0)
        mixing = (mixed * jnp.exp(gap) * step_t[h : h + 1, :]).astype(BFLOAT)
        y_o[:, h * size : (h + 1) * size] = nn(mixing, vals[:, h * size : (h + 1) * size])


def fold_in(me, count, payload, acc, reverse, heads):
    rows = acc.shape[0]
    size = rows // heads
    acc[...] = jnp.zeros_like(acc)
    for k in range(count):
        at = count - 1 - k if reverse else k
        reached = at > me if reverse else at < me

        @pl.when(reached)
        def _():
            keep = payload[at, rows : rows + 1]
            for h in range(heads):
                part = slice(h * size, (h + 1) * size)
                acc[part] = keep[:, h : h + 1] * acc[part] + payload[at, part]


def gated_kernel(
    flags, payload, local, retain, y, wr, vals, cum, meta, gate, misc, out_w, *rest, last_layer
):
    if last_layer:
        cot, got, ssm_o, states_o, partial_o, sums_o, cot_o, acc = rest
    else:
        ssm_o, states_o, partial_o, acc = rest
    b = pl.program_id(0)
    span, lanes = vals.shape
    heads = HEADS_OF(lanes)
    rows = acc.shape[0]
    size = rows // heads
    half = wr.shape[1] // 2

    @pl.when(b == 0)
    def _():
        fold_in(flags[0], payload.shape[0], payload, acc, False, heads)

    states = local[...] + acc[...]
    states_o[...] = states
    for h in range(heads):
        part = slice(h * size, (h + 1) * size)
        acc[part] = retain[0:1, h : h + 1] * acc[part]
    enter = meta[:, 3:4] * jnp.exp(cum[...])
    enter_lanes = nn(enter, spread_matrix(lanes, heads), PRECISE)
    carried = nt(wr[:, half:], states.astype(BFLOAT)) * enter_lanes
    ssm = y[...] + carried + misc[1:2] * vals[...].astype(FLOAT)
    ssm_o[...] = ssm
    gate_v = gate[...]
    gated = ssm * (gate_v * sigmoid(gate_v))
    partial = nn((gated * misc[0:1]).astype(BFLOAT), out_w[...])
    squares = nt(jnp.ones((8, lanes), FLOAT), gated * gated, PRECISE)
    if last_layer:
        partial_o[...] = partial
        sums_o[...] = jnp.zeros_like(sums_o)
        sums_o[0:1] = squares[0:1]
        given = jnp.where(flags[1] == 1, cot[...].astype(FLOAT), got[...])
        cot_o[...] = given
        sums_o[1:2] = nt(jnp.ones((8, partial.shape[1]), FLOAT), partial * given, PRECISE)[0:1]
    else:
        per = partial_o.shape[0] // 2
        inner = (per - EDGE) // span
        base = pl.multiple_of((b // inner) * per, EDGE)
        partial_o[pl.ds(pl.multiple_of(base + (b % inner) * span, EDGE), span)] = partial
        foot = pl.ds(pl.multiple_of(base + inner * span, EDGE), EDGE)

        @pl.when(b % inner == 0)
        def _():
            partial_o[foot] = jnp.zeros((EDGE, partial.shape[1]), FLOAT)

        for k in range(inner):

            @pl.when(b % inner == k)
            def _():
                partial_o[foot, k * span : (k + 1) * span] = squares


def ungate_kernel(flags, *refs, last_layer):
    if last_layer:
        (upstream, sums), refs = refs[:2], refs[2:]
    else:
        (cot, above_mine, above_other, above_x, above_gain, mine, other), refs = refs[:7], refs[7:]
    (normed, out_w, misc, gate, ssm, vals, wr, cum, meta, retain), refs = refs[:10], refs[10:]
    if not last_layer:
        (up_o, gain_o), refs = refs[:2], refs[2:]
    grad_ssm_o, gate_low_o, packed_o, small_o, later_o, pay_o, state, grad_gate_w_o, grad_out_w_o = refs
    b = pl.program_id(0)
    block = pl.num_programs(0) - 1 - b
    lanes = vals.shape[1]
    heads = HEADS_OF(lanes)
    rows = state.shape[0]
    size = rows // heads
    half = wr.shape[1] // 2

    @pl.when(b == 0)
    def _():
        state[...] = jnp.zeros_like(state)
        grad_out_w_o[...] = jnp.zeros_like(grad_out_w_o)
        grad_gate_w_o[...] = jnp.zeros_like(grad_gate_w_o)
        small_o[...] = jnp.zeros_like(small_o)
        pay_o[rows:] = jnp.ones_like(pay_o[rows:])
        if not last_layer:
            gain_o[...] = jnp.zeros_like(gain_o)

    if last_layer:
        up = upstream[...]
        sums_t = sums[...].T
        inv_norm = lax.rsqrt(sums_t[:, 0:1] / INNER + EPSILON)
        grad_inv = sums_t[:, 1:2]
    else:
        grad_normed, _, _ = summed(block, flags[2], above_mine, above_other)
        x = above_x[...]
        inv_rms = lax.rsqrt(jnp.mean(x * x, axis=1, keepdims=True) + EPSILON)
        scaled = x * inv_rms
        gain_o[0:1] += jnp.sum(grad_normed * scaled, axis=0, keepdims=True)
        inner = grad_normed * above_gain[...]
        up = cot[...] + inv_rms * (inner - scaled * jnp.mean(inner * scaled, axis=1, keepdims=True))
        up_o[...] = up
        branch, inv_norm = branch_of(block, flags[2], mine, other)
        grad_inv = jnp.sum(up * branch, axis=1, keepdims=True)

    grad_branch = (inv_norm * up).astype(BFLOAT)
    gate_v = gate[...]
    sigma = sigmoid(gate_v)
    gate_act = gate_v * sigma
    ssm_v = ssm[...]
    gated = ssm_v * gate_act
    gain = misc[0:1]
    out_in = (gated * gain).astype(BFLOAT)
    grad_out_w_o[...] += tn(out_in, grad_branch)
    grad_out_in = nt(grad_branch, out_w[...])
    small_o[0:1] += jnp.sum(grad_out_in * gated, axis=0, keepdims=True)
    grad_gated = grad_out_in * gain - (grad_inv * inv_norm * inv_norm * inv_norm / INNER) * gated
    grad_ssm = (grad_gated * gate_act).astype(BFLOAT)
    grad_ssm_o[...] = grad_ssm
    gate_low = (grad_gated * ssm_v * (sigma * (1.0 + gate_v * (1.0 - sigma)))).astype(BFLOAT)
    gate_low_o[...] = gate_low
    grad_gate_w_o[...] += tn(normed[...], gate_low)
    grad_wide = grad_ssm.astype(FLOAT)
    small_o[1:2] += jnp.sum(grad_wide * vals[...].astype(FLOAT), axis=0, keepdims=True)
    enter = meta[:, 3:4] * jnp.exp(cum[...])
    enter_lanes = nn(enter, spread_matrix(lanes, heads), PRECISE)
    pulls = tn((enter_lanes * grad_wide).astype(BFLOAT), wr[:, half:])
    later_o[...] = state[...]
    keep = retain[0:1]
    for h in range(heads):
        part = slice(h * size, (h + 1) * size)
        state[part] = keep[:, h : h + 1] * state[part] + pulls[part]
    pay_o[0:rows] = state[...]
    pay_o[rows:] = pay_o[rows:] * keep

    @pl.when(block == 0)
    def _():
        count = packed_o.shape[0]
        size = grad_gate_w_o.shape[0] // count
        half = size // 2
        for j in range(count):
            packed_o[j, 0:size] = grad_gate_w_o[j * size : (j + 1) * size]
            packed_o[j, size : size + half] = grad_out_w_o[j * half : (j + 1) * half, 0:lanes]
            packed_o[j, size + half :] = grad_out_w_o[j * half : (j + 1) * half, lanes:]


def unmix_kernel(
    flags, payload, later, retain, grad_ssm, vals, wr, cum, shifted, meta, seg_row, states, conv, pre, before, pre_halo,
    filt, misc,
    low_o, edge_o, step_low_o, spill_o, small_o, small2_o,
    acc, flows, ext,
):
    b = pl.program_id(0)
    blocks = pl.num_programs(0)
    span, lanes = vals.shape
    heads = HEADS_OF(lanes)
    rows = acc.shape[0]
    size = rows // heads
    half = wr.shape[1] // 2
    write, read = wr[:, :half], wr[:, half:]

    @pl.when(b == 0)
    def _():
        fold_in(flags[0], payload.shape[0], payload, acc, True, heads)
        small_o[...] = jnp.zeros_like(small_o)
        small2_o[...] = jnp.zeros_like(small2_o)
        for k in range(CONV - 1):
            ext[k, span:] = jnp.zeros_like(ext[k, span:])

    @pl.when(b > 0)
    def _():
        for k in range(CONV - 1):
            ext[k, span:] = ext[k, 0:EDGE]

    grad_next = later[...] + acc[...]
    keep = retain[0:1]
    states_v = states[...]
    spread = spread_matrix(lanes, heads)
    meet = jnp.sum(grad_next * states_v, axis=1, keepdims=True)
    grad_retain = tn(jnp.broadcast_to(meet, (rows, LANES)) * spread.T, jnp.ones((rows, 8), FLOAT), PRECISE)
    grad_retain = grad_retain.T[0:1]
    for h in range(heads):
        part = slice(h * size, (h + 1) * size)
        acc[part] = keep[:, h : h + 1] * acc[part]

    cum_v = cum[...]
    cum_t = cum_v.T
    shifted_v = shifted[...]
    steps = softplus(shifted_v)
    step_t = steps.T
    seg_mask = within_block(meta[:, 5:6], seg_row[...])
    inter = jnp.where(seg_mask, nt(read, write), 0.0)
    grad_inter = jnp.zeros((span, span), FLOAT)
    flows[...] = jnp.zeros_like(flows)
    parts = []
    row_sums = jnp.zeros((span, LANES), FLOAT)
    lane_no = lax.broadcasted_iota(jnp.int32, (span, LANES), 1)
    for h in range(heads):
        part = slice(h * size, (h + 1) * size)
        decay = jnp.exp(jnp.where(seg_mask, cum_v[:, h : h + 1] - cum_t[h : h + 1, :], 0.0))
        decay_inter = decay * inter
        step_h = step_t[h : h + 1, :]
        mixing = (decay_inter * step_h).astype(BFLOAT)
        grad_h = grad_ssm[:, part]
        parts.append(tn(mixing, grad_h))
        pairing = nt(grad_h, vals[:, part])
        grad_inter = grad_inter + pairing * decay * step_h
        weighted = pairing * decay_inter
        col = jnp.sum(weighted, axis=0, keepdims=True)
        flows[h : h + 1, :] = col
        row_sums = row_sums + jnp.where(
            lane_no == h, jnp.sum(weighted * step_h, axis=1, keepdims=True), 0.0
        )
    grad_vals = jnp.concatenate(parts, axis=1)
    grad_steps = flows[...].T
    grad_cum = row_sums - grad_steps * steps
    grad_inter = jnp.where(seg_mask, grad_inter, 0.0).astype(BFLOAT)
    grad_read = nn(grad_inter, write)
    grad_write = tn(grad_inter, read)

    vals_f = vals[...].astype(FLOAT)
    grad_f = grad_ssm[...].astype(FLOAT)
    enter = meta[:, 3:4] * jnp.exp(cum_v)
    enter_lanes = nn(enter, spread, PRECISE)
    states_low = states_v.astype(BFLOAT)
    grad_read = grad_read + nn((enter_lanes * grad_f).astype(BFLOAT), states_low)
    out_of = nt(read, states_low)
    grad_cum = grad_cum + enter * nt(grad_f * out_of, spread, PRECISE)
    next_low = grad_next.astype(BFLOAT)
    along = nt(write, next_low)
    last = cum_v[span - 1 : span]
    tail = meta[:, 4:5] * jnp.exp(last - cum_v)
    tail_step = tail * steps
    tail_lanes = nn(tail_step, spread, PRECISE)
    grad_vals = grad_vals + tail_lanes * along + misc[1:2] * grad_f
    grad_write = grad_write + nn((tail_lanes * vals_f).astype(BFLOAT), next_low)
    reach = nt(vals_f * along, spread, PRECISE)
    grad_steps = grad_steps + tail * reach
    tail_flow = tail_step * reach
    grad_last = jnp.sum(tail_flow, axis=0, keepdims=True) + grad_retain * keep
    grad_log = nn(triangle(span, True), grad_cum - tail_flow, PRECISE) + grad_last
    rate_v = misc[3:4, 0:LANES]
    log_decay = -rate_v * steps
    small2_o[0:1] += jnp.sum(grad_log * log_decay, axis=0, keepdims=True)
    grad_shifted = (grad_steps - rate_v * grad_log) * sigmoid(shifted_v)
    small2_o[1:2] += jnp.sum(grad_shifted, axis=0, keepdims=True)
    step_low_o[...] = grad_shifted.astype(BFLOAT)

    grad_conv = jnp.concatenate([grad_vals, grad_write, grad_read], axis=1) * silu_slope(conv[...])
    small_o[CONV : CONV + 1] += jnp.sum(grad_conv, axis=0, keepdims=True)
    pre_v = pre[...]
    small_o[CONV - 1 : CONV] += jnp.sum(grad_conv * pre_v, axis=0, keepdims=True)
    grad_pre = filt[CONV - 1 : CONV] * grad_conv
    first = blocks - 1 - b == 0
    for k in range(CONV - 1):
        lag = CONV - 1 - k
        masked = grad_conv * meta[:, k : k + 1]
        ext[k, 0:span] = masked
        ahead = ext[k, lag : lag + span]
        row_no = lax.broadcasted_iota(jnp.int32, (span, 1), 0)
        own = jnp.where(row_no < span - lag, ahead, 0.0)
        edge = jnp.where(first, pre_halo[...], before[...])
        head_rows = ext[k, 0:EDGE]
        edge_sum = jnp.zeros((1, head_rows.shape[1]), FLOAT)
        for t in range(lag):
            edge_sum = edge_sum + head_rows[t : t + 1] * edge[EDGE - lag + t : EDGE - lag + t + 1]
        small_o[k : k + 1] += jnp.sum(own * pre_v, axis=0, keepdims=True) + edge_sum
        grad_pre = grad_pre + filt[k : k + 1] * ahead
    low_o[...] = grad_pre.astype(BFLOAT)

    @pl.when(b == 0)
    def _():
        edge_o[...] = grad_pre[span - EDGE :]

    spill_o[...] = jnp.zeros_like(spill_o)
    for k in range(CONV - 1):
        lag = CONV - 1 - k
        for t in range(lag):
            at = EDGE - lag + t
            spill_o[at : at + 1] += filt[k : k + 1] * ext[k, t : t + 1]


def common_places(count, size):
    for j in range(count):
        for group in range(3):
            at = group * count * size + j * size
            side, row = divmod(at, 3 * count * size // 2)
            yield j, group, side, row


def weights_kernel(
    normed, low, edge, spill, gate_low, step_low, gate_w, value_w, state_w, step_w,
    small, small_c, small_h,
    grad_normed_o, packed_o,
    value_a, common_a, step_a,
):
    b = pl.program_id(0)
    blocks = pl.num_programs(0)
    span = low.shape[0]
    lanes = value_w.shape[1]
    d = value_w.shape[0]

    @pl.when(b == 0)
    def _():
        value_a[...] = jnp.zeros_like(value_a)
        common_a[...] = jnp.zeros_like(common_a)
        step_a[...] = jnp.zeros_like(step_a)

    patch = edge[...] + spill[...]
    padded = jnp.concatenate([jnp.zeros((span - EDGE, patch.shape[1]), FLOAT), patch], axis=0)
    row_no = lax.broadcasted_iota(jnp.int32, (span, 1), 0)
    use = (row_no >= span - EDGE) & (b == blocks - 1)
    low_v = jnp.where(use, padded, low[...].astype(FLOAT)).astype(BFLOAT)
    value_low, state_low = low_v[:, :lanes], low_v[:, lanes:]
    normed_v = normed[...]
    value_a[...] += tn(normed_v, value_low)
    common_a[0:d] += tn(normed_v, state_low)
    step_a[...] += tn(step_low[...], normed_v)
    grad_normed_o[...] = (
        nt(gate_low[...], gate_w[...])
        + nt(value_low, value_w[...])
        + nt(state_low, state_w[...])
        + nn(step_low[...], step_w[...])
    )

    @pl.when(b == blocks - 1)
    def _():
        common_a[d : d + EDGE] = small_c[0:EDGE, lanes:]
        count = packed_o.shape[0]
        size = d // count
        rows = size
        for j in range(count):
            packed_o[j, 0:size] = value_a[j * size : (j + 1) * size]
        packed_o[0, rows : rows + 5] = small_c[0:5, 0:lanes]
        packed_o[0, rows + 5 : rows + 7] = small[0:2]
        packed_o[0, rows + 7 : rows + 8, 0:LANES] = small_h[0:1]
        packed_o[0, rows + 7 : rows + 8, LANES : 2 * LANES] = small_h[1:2]
        packed_o[0, rows + 7 : rows + 8, 2 * LANES :] = jnp.zeros((1, lanes - 2 * LANES), FLOAT)
        packed_o[1, rows : rows + 8] = jnp.zeros((8, lanes), FLOAT)
        packed_o[2, rows : rows + 8] = step_a[0:8, 0:lanes]
        packed_o[3, rows : rows + 8] = step_a[0:8, lanes:]
        rows += 8
        part = packed_o.shape[1] - rows
        for j, group, side, row in common_places(count, part):
            packed_o[j, rows:, group * LANES : (group + 1) * LANES] = common_a[
                row : row + part, side * LANES : (side + 1) * LANES
            ]


AXES = ("dp", "ctx", "tensor")


def move(shard, dest):
    sizes = [lax.axis_size(axis) for axis in AXES]
    pairs = []
    for dp in range(sizes[0]):
        for q in range(sizes[1]):
            for t in range(sizes[2]):
                to = dest(dp, q, t)
                if to is not None:
                    pairs.append(
                        ((dp * sizes[1] + q) * sizes[2] + t, (to[0] * sizes[1] + to[1]) * sizes[2] + to[2])
                    )
    return lax.ppermute(shard, AXES, pairs)


def other_core(dp, q, t):
    return dp ^ 1, q, t


def beside(dp, q, t):
    return dp, q, t ^ 1


def at_home(dp, t):
    return t // 2 == dp % 2


class Where:
    def __init__(self):
        self.core = lax.axis_index("dp") % 2
        self.q = lax.axis_index("ctx")
        self.t = lax.axis_index("tensor")
        self.high = self.t // 2
        self.low = self.t % 2
        self.home = self.core == self.high
        self.count = lax.axis_size("ctx")
        self.flags = jnp.stack([self.q, self.home, self.core, self.t]).astype(jnp.int32)
        self.outer = lax.axis_size("dp") // 2


def piece(array, at, count):
    size = array.shape[0] // count
    return lax.dynamic_slice_in_dim(array, at * size, size)


def in_order(w, pieces):
    size = pieces[0].shape[0]
    full = jnp.zeros((size * len(pieces),) + pieces[0].shape[1:], pieces[0].dtype)
    for k, part in enumerate(pieces):
        full = lax.dynamic_update_slice_in_dim(full, part, (w.q ^ k) * size, 0)
    return full


def from_core(w, array):
    got = move(array, lambda dp, q, t: (dp ^ 1, q, t) if at_home(dp, t) else None)
    return jnp.where(w.home, array, got)


def tie(w, array, event):
    first = event[(0,) * event.ndim].astype(array.dtype)
    return array + jnp.where(w.q > 1000, first, jnp.zeros_like(first))


def event_of(*arrays):
    return sum(array[(0,) * array.ndim].astype(FLOAT) for array in arrays).reshape(1, 1)


def pack_kernel(flags, value, gate, out, taps, off, gain, bias, decay, skip, step, *outs, layers):
    lanes = value.shape[2]
    d = value.shape[1]
    size = d // 4
    half = size // 2
    heads = step.shape[2]
    for l, parts in layers:
        places = [(outs[number], at) for number, at in parts]
        (first, base), (second, then) = places
        rows = pl.ds(pl.multiple_of(flags[0] * size, size), size)
        first[base : base + size] = value[l, rows].astype(FLOAT)
        base += size
        first[base : base + 16] = jnp.zeros((16, lanes), FLOAT)
        first[base : base + CONV] = taps[l]
        first[base + CONV : base + CONV + 1] = off[l : l + 1]
        first[base + CONV + 1 : base + CONV + 2] = gain[l : l + 1]
        first[base + 6 : base + 7, 0:heads] = bias[l : l + 1]
        first[base + 7 : base + 8, 0:heads] = decay[l : l + 1]
        first[base + 8 : base + 9, 0:heads] = skip[l : l + 1]
        wide = jnp.concatenate([step[l].astype(FLOAT), jnp.zeros((d, LANES - heads), FLOAT)], axis=1).T
        first[base + 16 : base + 24] = wide[0:8, 0:lanes]
        first[base + 24 : base + 32] = wide[0:8, lanes:]
        second[then : then + size] = gate[l, rows].astype(FLOAT)
        half_rows = pl.ds(pl.multiple_of(flags[0] * half, half), half)
        wide = out[l, half_rows].astype(FLOAT)
        second[then + size : then + size + half] = wide[:, 0:lanes]
        second[then + size + half : then + 2 * size] = wide[:, lanes:]


def value_kernel(flags, value, own, state_taps, state_off, *rest, layer):
    pieces, (value_o, step_o, filt_o, misc_o) = rest[:-4], rest[-4:]
    d, lanes = value_o.shape
    size = d // len(pieces)
    heads = HEADS_OF(lanes)

    @pl.when(flags[1] == 1)
    def _():
        value_o[...] = value[...]

    @pl.when(flags[1] == 0)
    def _():
        for k, part in enumerate(pieces):
            at = pl.multiple_of((flags[0] ^ k) * size, size)
            value_o[pl.ds(at, size)] = part[0:size].astype(BFLOAT)

    small = jnp.where(flags[1] == 1, own[size : size + 32], pieces[0][size : size + 32])
    step_o[...] = jnp.zeros_like(step_o)
    step_o[0:16, 0:lanes] = jnp.concatenate([small[16:24], jnp.zeros((8, lanes), FLOAT)]).astype(BFLOAT)
    step_o[0:16, lanes:] = jnp.concatenate([small[24:32], jnp.zeros((8, lanes), FLOAT)]).astype(BFLOAT)
    filt_o[...] = jnp.zeros_like(filt_o)
    filt_o[0 : CONV + 1, 0:lanes] = small[0 : CONV + 1]
    filt_o[0:CONV, lanes:] = state_taps[layer]
    filt_o[CONV : CONV + 1, lanes:] = state_off[layer : layer + 1]
    misc_o[...] = jnp.zeros_like(misc_o)
    misc_o[0:1] = small[CONV + 1 : CONV + 2]
    skip = jnp.broadcast_to(small[8:9, 0:LANES], (8, LANES))
    misc_o[1:2] = nn(skip, spread_matrix(lanes, heads), PRECISE)[0:1]
    misc_o[2:3, 0:LANES] = small[6:7, 0:LANES]
    lane_no = lax.broadcasted_iota(jnp.int32, (1, LANES), 1)
    misc_o[3:4, 0:LANES] = jnp.where(lane_no < heads, jnp.exp(small[7:8, 0:LANES]), 0.0)


def gate_kernel(flags, gate, out, *rest, base):
    pieces, (gate_o, out_o) = rest[:-2], rest[-2:]
    d, lanes = gate_o.shape
    size = d // len(pieces)
    half = size // 2

    @pl.when(flags[1] == 1)
    def _():
        gate_o[...] = gate[...]
        out_o[...] = out[...]

    @pl.when(flags[1] == 0)
    def _():
        for k, part in enumerate(pieces):
            at = pl.multiple_of((flags[0] ^ k) * size, size)
            gate_o[pl.ds(at, size)] = part[base : base + size].astype(BFLOAT)
            at = pl.multiple_of((flags[0] ^ k) * half, half)
            out_o[pl.ds(at, half), 0:lanes] = part[base + size : base + size + half].astype(BFLOAT)
            out_o[pl.ds(at, half), lanes:] = part[base + size + half : base + 2 * size].astype(BFLOAT)


def fetch_part(packed):
    return move(packed, lambda dp, q, t: (dp, q, t ^ 2) if at_home(dp, t) else None)


def fetch_rest(w, part):
    return [part] + [
        move(part, lambda dp, q, t, k=k: None if at_home(dp, t) else (dp, q ^ k, t)) for k in range(1, w.count)
    ]


def layer_spec(shape, layer):
    return pl.BlockSpec((None,) + tuple(shape[1:]), lambda b: (layer,) + (0,) * (len(shape) - 1))


def delivered_kernel(flags, own, got, *rest, last):
    if last:
        (
            gate_o, value_o, out_o, rows_o, state_o, gain_in_o, step_o, taps_o, off_o, state_taps_o, state_off_o,
            bias_o, decay_o, skip_o, gain_o, wide,
        ) = rest[-16:]
        rows_1 = rest[0]
    else:
        gate_o, value_o, out_o, rows_o = rest
    count = own.shape[0]
    d, lanes = value_o.shape
    size = d // count
    half = size // 2
    rows = 3 * size
    part = (own.shape[1] - rows - 16) // LAYERS

    def put(source):
        for j in range(count):
            k = flags[0] ^ j
            gate_o[j * size : (j + 1) * size] = source[k, 0:size]
            out_o[j * half : (j + 1) * half, 0:lanes] = source[k, size : size + half]
            out_o[j * half : (j + 1) * half, lanes:] = source[k, size + half : 2 * size]
            value_o[j * size : (j + 1) * size] = source[k, 2 * size : rows]
            rows_o[j * 8 : (j + 1) * 8] = source[k, rows : rows + 8]
        if last:
            total = jnp.zeros((8, lanes), FLOAT)
            for j in range(count):
                total = total + source[j, rows + 8 + LAYERS * part :]
            for l in range(LAYERS):
                for k in range(d // lanes):
                    at = l * (d // lanes) + k
                    gain_in_o[l : l + 1, k * lanes : (k + 1) * lanes] = total[at : at + 1]
                base = rows + 8 + l * part
                for j, group, side, row in common_places(count, part):
                    wide[row : row + part, side * LANES : (side + 1) * LANES] = source[
                        flags[0] ^ j, base : base + part, group * LANES : (group + 1) * LANES
                    ]
                state_o[l] = wide[0:d]
                state_taps_o[l] = wide[d : d + CONV]
                state_off_o[l : l + 1] = wide[d + CONV : d + CONV + 1]

    @pl.when(flags[1] == 1)
    def _():
        put(own)

    @pl.when(flags[1] == 0)
    def _():
        put(got)

    if last:
        heads = bias_o.shape[1]
        spread = spread_matrix(lanes, heads)
        for l, mine in ((0, rows_o), (1, rows_1)):
            taps_o[l] = mine[0:CONV]
            off_o[l : l + 1] = mine[CONV : CONV + 1]
            gain_o[l : l + 1] = mine[CONV + 1 : CONV + 2]
            skip = nt(mine[0:8], spread, PRECISE)
            skip_o[l : l + 1] = skip[6:7, 0:heads]
            decay_o[l : l + 1] = mine[7:8, 0:heads]
            bias_o[l : l + 1] = mine[7:8, LANES : LANES + heads]
            step_o[l, 0:lanes] = mine[16:24].T[:, 0:heads]
            step_o[l, lanes:] = mine[24:32].T[:, 0:heads]


def joined_kernel(flags, have, got, out):
    own = pl.program_id(0) == flags[2]

    @pl.when(own)
    def _():
        out[...] = have[...].astype(BFLOAT)

    @pl.when(jnp.logical_not(own))
    def _():
        out[...] = got[...].astype(BFLOAT)


def halves(w, array):
    return piece(array, w.core, 2) + move(piece(array, 1 - w.core, 2), other_core)


def add_up(w, array, tied=None):
    first = halves(w, array)
    got = move(first, beside)
    part = first + (tied(first, got) if tied else got)
    return first, part, move(part, other_core)


def add_small(array):
    array = array + move(array, other_core)
    return array + move(array, beside)


def add_rows(w, array):
    part = halves(w, array)
    return piece(part, w.low, 2) + move(piece(part, 1 - w.low, 2), beside)


def hand_step(w, up, down):
    count = lax.axis_size("tensor")
    return (
        move(up, lambda dp, q, t: (dp, q, t + 1) if t + 1 < count else None),
        move(down, lambda dp, q, t: (dp, q, t - 1) if t > 0 else None),
    )


def hand_out(w, rows):
    up, down, steps = rows, rows, []
    for _ in range(lax.axis_size("tensor") - 1):
        up, down = hand_step(w, up, down)
        steps.append((up, down))
        up, down = tie(w, up, down), tie(w, down, up)
    return steps


def hand_out_end(w, rows, steps):
    def unit(j):
        total = jnp.where(w.t == j, rows, 0.0)
        for k, (up, down) in enumerate(steps, 1):
            total = jnp.where(w.t == j + k, up, jnp.where(w.t == j - k, down, total))
        return total

    units = [unit(j) for j in range(len(steps) + 1)]
    low, high = jnp.concatenate(units[:2]), jnp.concatenate(units[2:])
    have = jnp.where(w.core == 0, low, high)
    got = move(jnp.where(w.core == 0, high, low), other_core)
    (out,) = call(
        joined_kernel, 2,
        [(w.flags, "smem"), (have, "whole"), (got, "whole")],
        [((2 * have.shape[0], have.shape[1]), BFLOAT, "rows")],
    )
    return out, got


def over_outer(w, part):
    total = part
    for k in range(1, w.outer):
        size = 2 * w.outer
        total = total + move(part, lambda dp, q, t, k=k: ((dp + 2 * k) % size, q, t))
    return total


def total_start(w, packed, event):
    def at(k):
        return tie(w, lax.dynamic_index_in_dim(packed, w.q ^ k, 0, keepdims=False), event)

    return [at(0)] + [move(at(k), lambda dp, q, t, k=k: (dp, q ^ k, t)) for k in range(1, w.count)]


def across(array):
    return move(array, lambda dp, q, t: None if at_home(dp, t) else (dp, q, t ^ 2))


def total_spread(w, part):
    got = [
        move(part, lambda dp, q, t, k=k: (dp, q ^ k, t) if at_home(dp, t) else None) for k in range(1, w.count)
    ]
    return part, got


def total_end(w, layer, part, got, shapes, before, small=()):
    own = jnp.stack([part] + got)
    got = move(own, lambda dp, q, t: (dp ^ 1, q, t) if at_home(dp, t) else None)
    last = before is not None
    inputs = [(w.flags, "smem"), (own, "whole"), (got, "whole")]
    outputs = [(shape, FLOAT, layer_spec(shape, layer)) for shape in shapes]
    outputs.append(((32, shapes[0][2]), FLOAT, "whole"))
    aliases, scratch = {}, []
    if last:
        inputs.append((before[-1], "whole"))
        aliases = {len(inputs) + i: i for i in range(len(shapes))}
        inputs += [(array, pl.BlockSpec(memory_space=pl.ANY)) for array in before[:-1]]
        outputs += [(shape, FLOAT, "whole") for shape in small]
        d = shapes[0][1]
        part = (own.shape[1] - 3 * d // 4 - 16) // LAYERS
        scratch = [pltpu.VMEM((6 * part, small[0][2]), FLOAT)]
    return call(
        functools.partial(delivered_kernel, last=last), 1, inputs, outputs, scratch, aliases=aliases
    )


def passed_along(shard, axis, by):
    count = lax.axis_size(axis)
    pairs = [(i, i + by) for i in range(count) if 0 <= i + by < count]
    return lax.ppermute(shard, axis, pairs)


def forward_layer(w, source, wts, geometry, given=None, deps=(), then=lambda event: ()):
    meta, seg_row = geometry
    first = len(source) == 3
    n, d = source[0].shape
    grid = n // GROUP
    lanes = wts["value_w"].shape[1]
    wide = wts["state_w"].shape[1]
    chans = lanes + wide
    state = wide // 2
    pay = (lanes + 8, state)
    if first:
        got = pl.BlockSpec((GROUP, d), lambda b: (b, 0))
        entry = [(source[0], "rows"), (source[1], got), (source[2], "whole")]
    else:
        entry = [(source[0], "rows")] + [(array, "whole") for array in source[1:]]
    x, normed, pre, pre_halo, conv, vals, wr, shifted, cum, local, retain, payload = call(
        functools.partial(project_kernel, first_layer=first), grid,
        [(w.flags, "smem")] + entry + [
            (wts["gain"], "whole"), (wts["value_w"], "whole"), (wts["state_w"], "whole"), (wts["step_w"], "whole"),
            (wts["filt"], "whole"), (wts["misc"], "whole"), (meta, "rows"),
        ],
        [
            ((n, d), FLOAT, "rows"), ((n, d), BFLOAT, "rows"), ((n, chans), FLOAT, "rows"),
            ((EDGE, chans), FLOAT, "whole"), ((n, chans), FLOAT, "rows"), ((n, lanes), BFLOAT, "rows"),
            ((n, wide), BFLOAT, "rows"), ((n, LANES), FLOAT, "rows"), ((n, LANES), FLOAT, "rows"),
            ((grid, lanes, state), FLOAT, "lead"), ((grid, 8, LANES), FLOAT, "lead"), (pay, FLOAT, "whole"),
        ],
        [pltpu.VMEM((GROUP + EDGE, chans), FLOAT), pltpu.VMEM((lanes, state), FLOAT)],
        flops=2 * n * d * chans,
        deps=deps,
    )
    everything = lax.all_gather(payload, "ctx")
    gate_w, out_w = wts["late"](payload)
    gate, y = call(
        inside_kernel, grid,
        [(normed, "rows"), (gate_w, "whole"), (vals, "rows"), (wr, "rows"), (cum, "rows"),
         (shifted, "rows"), (meta, "rows"), (seg_row, "lead")],
        [((n, lanes), FLOAT, "rows"), ((n, lanes), FLOAT, "rows")],
        flops=4 * n * GROUP * lanes,
        deps=then(payload),
    )
    last = given is not None
    extra = [(given[0], "rows"), (given[1], "rows")] if last else []
    if last:
        results = [((n, d), FLOAT, "rows"), ((grid, 8, GROUP), FLOAT, "lead"), ((n, d), FLOAT, "rows")]
    else:
        results = [((n + 2 * EDGE, d), FLOAT, "whole")]
    outs = call(
        functools.partial(gated_kernel, last_layer=last), grid,
        [
            (w.flags, "smem"), (everything, "whole"), (local, "lead"), (retain, "lead"), (y, "rows"), (wr, "rows"),
            (vals, "rows"), (cum, "rows"), (meta, "rows"), (gate, "rows"), (wts["misc"], "whole"), (out_w, "whole"),
        ] + extra,
        [((n, lanes), FLOAT, "rows"), ((grid, lanes, state), FLOAT, "lead")] + results,
        [pltpu.VMEM((lanes, state), FLOAT)],
        flops=2 * n * d * lanes,
    )
    ssm, states = outs[0], outs[1]
    saved = (normed, gate, pre, pre_halo, conv, vals, wr, shifted, cum, retain, ssm, states, gate_w, out_w)
    return x, outs[2:], saved


def backward_layer(w, source, wts, saved, geometry, deps):
    meta, seg_row = geometry
    normed, gate, pre, pre_halo, conv, vals, wr, shifted, cum, retain, ssm, states, gate_w, out_w = saved
    last = len(source) == 2
    n, d = source[0].shape
    grid = n // GROUP
    lanes = vals.shape[1]
    chans = pre.shape[1]
    state = wr.shape[1] // 2
    pay = (lanes + 8, state)
    if last:
        entry = [(source[0], "rows"), (source[1], "lead")]
        above = []
    else:
        kinds = ["rows", "whole", "whole", "rows", "whole", "whole", "whole"]
        entry = list(zip(source, kinds))
        above = [((n, d), FLOAT, "rows"), ((8, d), FLOAT, "whole")]
    outs = call(
        functools.partial(ungate_kernel, last_layer=last), grid,
        [(w.flags, "smem")] + entry + [
            (normed, "rows"), (out_w, "whole"), (wts["misc"], "whole"), (gate, "rows"), (ssm, "rows"),
            (vals, "rows"), (wr, "rows"), (cum, "rows"), (meta, "rows"), (retain, "lead"),
        ],
        above + [
            ((n, lanes), BFLOAT, "rows"), ((n, lanes), BFLOAT, "rows"), ((4, d // 2, lanes), FLOAT, "whole"),
            ((8, lanes), FLOAT, "whole"), ((grid, lanes, state), FLOAT, "lead"), (pay, FLOAT, "whole"),
        ],
        [pltpu.VMEM((lanes, state), FLOAT), pltpu.VMEM((d, lanes), FLOAT), pltpu.VMEM((lanes, d), FLOAT)],
        reverse=True,
        flops=6 * n * d * lanes,
        deps=deps[0],
    )
    above = outs[: len(above)]
    grad_ssm, gate_low, packed_a, small, later, payload = outs[len(above) :]
    everything = lax.all_gather(payload, "ctx")
    got_a = total_start(w, packed_a, everything)
    strip = GROUP // EDGE
    before = pl.BlockSpec((EDGE, chans), lambda b: (jnp.maximum((grid - 1 - b) * strip - 1, 0), 0))
    low, edge, step_low, spill, small_c, small_h = call(
        unmix_kernel, grid,
        [
            (w.flags, "smem"), (everything, "whole"), (later, "lead"), (retain, "lead"), (grad_ssm, "rows"),
            (vals, "rows"), (wr, "rows"), (cum, "rows"), (shifted, "rows"), (meta, "rows"), (seg_row, "lead"),
            (states, "lead"), (conv, "rows"), (pre, "rows"), (pre, before), (pre_halo, "whole"),
            (wts["filt"], "whole"), (wts["misc"], "whole"),
        ],
        [
            ((n, chans), BFLOAT, "rows"), ((EDGE, chans), FLOAT, "whole"), ((n, LANES), BFLOAT, "rows"),
            ((EDGE, chans), FLOAT, "whole"), ((8, chans), FLOAT, "whole"), ((8, LANES), FLOAT, "whole"),
        ],
        [
            pltpu.VMEM((lanes, state), FLOAT), pltpu.VMEM((LANES, GROUP), FLOAT),
            pltpu.VMEM((CONV - 1, GROUP + EDGE, chans), FLOAT),
        ],
        reverse=True,
        flops=12 * n * GROUP * lanes,
        deps=deps[1](payload),
    )
    spill = passed_along(spill, "ctx", -1)
    part_a = over_outer(w, sum(got_a[1:], got_a[0]))
    common = 144
    grad_normed, packed = call(
        weights_kernel, grid,
        [
            (normed, "rows"), (low, "rows"), (edge, "whole"), (spill, "whole"), (gate_low, "rows"),
            (step_low, "rows"), (gate_w, "whole"), (wts["value_w"], "whole"), (wts["state_w"], "whole"),
            (wts["step_w"], "whole"), (small, "whole"),
            (small_c, "whole"), (small_h, "whole"),
        ],
        [((n, d), FLOAT, "rows"), ((4, d // 4 + 8 + common, lanes), FLOAT, "whole")],
        [pltpu.VMEM((d, lanes), FLOAT), pltpu.VMEM((6 * common, chans - lanes), FLOAT), pltpu.VMEM((LANES, d), FLOAT)],
        flops=4 * n * d * (lanes + chans),
        deps=deps[2](low) + [part_a],
    )
    return grad_normed, (part_a, packed), above


def local(tokens, segments, *rest):
    params, cotangent = rest[:-1], rest[-1]
    (
        in_gain, gate_w, value_w, state_w, step_w, value_filt, value_off, state_filt, state_off,
        bias_step, decay_param, skip_param, gain_out, out_w,
    ) = params
    n, d = tokens.shape
    w = Where()
    heads = step_w.shape[2]
    lanes = value_w.shape[2]
    wide = state_w.shape[2]
    size = d // w.count

    def pack(layers, shapes, deps=()):
        return call(
            functools.partial(pack_kernel, layers=layers), 1,
            [(w.flags, "smem")] + [
                (array, "whole") for array in (
                    value_w, gate_w, out_w, value_filt, value_off, gain_out, bias_step, decay_param, skip_param, step_w
                )
            ],
            [(shape, FLOAT, "whole") for shape in shapes],
            deps=deps,
        )

    def early(l, own, pieces):
        value, step, filt, misc = call(
            functools.partial(value_kernel, layer=l), 1,
            [(w.flags, "smem"), (value_w, layer_spec(value_w.shape, l)), (own, "whole"), (state_filt, "whole"),
             (state_off, "whole")] + [(part, "whole") for part in pieces],
            [((d, lanes), BFLOAT, "whole"), ((LANES, d), BFLOAT, "whole"), ((8, lanes + wide), FLOAT, "whole"),
             ((8, lanes), FLOAT, "whole")],
        )
        return dict(gain=in_gain[l][None], value_w=value, step_w=step, state_w=state_w[l], filt=filt, misc=misc)

    def late(l, pieces, base, deps=()):
        return call(
            functools.partial(gate_kernel, base=base), 1,
            [(w.flags, "smem"), (gate_w, layer_spec(gate_w.shape, l)), (out_w, layer_spec(out_w.shape, l))]
            + [(part, "whole") for part in pieces],
            [((d, lanes), BFLOAT, "whole"), ((lanes, d), BFLOAT, "whole")],
            deps=deps,
        )

    near = (size + 32, lanes)
    far = (2 * size, lanes)
    both = (near[0] + far[0], lanes)
    pack_a, pack_b, pack_1 = pack(((0, ((0, 0), (1, 0))), (1, ((2, 0), (2, near[0])))), (near, far, both))
    part_a = fetch_part(pack_a)
    edge = jnp.concatenate([
        tokens[n - EDGE :].astype(FLOAT),
        jnp.pad(segments[n - EDGE :].astype(FLOAT)[None], ((0, EDGE - 1), (0, d - EDGE))),
    ])
    edge = passed_along(edge, "ctx", 1)
    segs = jnp.pad(segments.astype(FLOAT), (0, 8 * d - n)).reshape(8, d)
    body = jnp.concatenate([tokens.astype(FLOAT), segs])
    body = move(body, lambda dp, q, t: (dp ^ 1, q, t) if at_home(dp, t) else None)
    part_b = fetch_part(tie(w, pack_b, part_a))
    edge = from_core(w, edge)
    segs = jnp.where(w.home, segs, body[n:]).reshape(-1)[:n]
    seg_ext = jnp.concatenate([edge[EDGE, :EDGE], segs])
    seg_blocks = segs.reshape(-1, GROUP)
    seg_before = jnp.concatenate([seg_ext[EDGE - 1 : EDGE], seg_blocks[:-1, -1]])
    first = EDGE - (CONV - 1)
    columns = [seg_ext[first + k : first + k + n] == segs for k in range(CONV - 1)]
    columns.append((seg_blocks == seg_before[:, None]).reshape(n))
    columns.append((seg_blocks == seg_blocks[:, -1:]).reshape(n))
    columns.append(segs)
    columns += [jnp.zeros_like(segs)] * (8 - len(columns))
    meta = jnp.stack([column.astype(FLOAT) for column in columns], axis=1)
    geometry = (meta, segs.reshape(-1, 1, GROUP))

    wts = [early(0, pack_a, fetch_rest(w, part_a))]
    wts[0]["late"] = lambda event: late(0, fetch_rest(w, part_b), 0, [event])
    halo = edge[:EDGE]
    sent = {"pack": pack_1}

    def send_next(event):
        sent["part"] = fetch_part(tie(w, sent["pack"], part_b))
        return [sent["part"]]

    x_0, (partial,), saved_0 = forward_layer(
        w, (tokens, body, halo), wts[0], geometry, deps=[part_b], then=send_next
    )

    def meanwhile(first, got):
        pieces = fetch_rest(w, tie(w, sent["part"], first))
        wts.append(early(1, sent["pack"], pieces))
        wts[1]["late"] = lambda event: late(1, pieces, near[0])
        sent["cot"] = move(
            tie(w, cotangent.astype(FLOAT), first),
            lambda dp, q, t: (dp ^ 1, q, t) if at_home(dp, t) else None,
        )
        return tie(w, got, wts[1]["misc"])

    _, mine, other = add_up(w, partial, meanwhile)
    edge_1 = mine[mine.shape[0] - 2 * EDGE :]
    from_last = [
        move(edge_1, lambda dp, q, t, c=c: (dp - 1 + c, q + 1, t) if dp % 2 == 1 and q + 1 < w.count else None)
        for c in (0, 1)
    ]
    edge_1 = from_last[0] + from_last[1]

    x_1, (partial, sums, cot), saved_1 = forward_layer(
        w, (x_0, mine, other, halo, edge_1), wts[1], geometry, (cotangent, sent["cot"])
    )
    sums = add_small(sums)
    quarter = 2 * w.core + w.low
    half = halves(w, partial)
    branch = piece(half, w.low, 2) + move(tie(w, piece(half, 1 - w.low, 2), sums), beside)
    rows_sq = lax.dynamic_index_in_dim(sums, quarter, 0, keepdims=False)[0]
    mixed = piece(x_1, quarter, 4) + lax.rsqrt(rows_sq / INNER + EPSILON)[:, None] * branch
    mixed_first = hand_step(w, mixed, mixed)

    grad_normed, packed, _ = backward_layer(
        w, (cot, sums), wts[1], saved_1, geometry,
        ([half], lambda event: [mixed], lambda event: list(mixed_first)),
    )
    held = {}

    def gather(first, got):
        held["start"] = total_start(w, packed[1], first)
        held["start"] = sum(held["start"][1:], held["start"][0])
        return tie(w, got, held["start"])

    _, above_mine, above_other = add_up(w, grad_normed, gather)
    part_1 = packed[0]
    shard_rows = size + 8
    none = jnp.zeros((8, lanes), FLOAT)

    shapes = (
        (LAYERS, d, lanes), (LAYERS, d, lanes), (LAYERS, lanes, d),
    )

    def middle(event):
        held["main"] = tie(w, jnp.concatenate([part_1, held["start"][:shard_rows]]), event)
        held["far"] = across(held["main"])
        up, down = (tie(w, array, event) for array in mixed_first)
        up, down = held["second"] = hand_step(w, up, down)
        held["third"] = hand_step(w, tie(w, up, down), tie(w, down, up))
        return [held["main"], up, down]

    def spread(event):
        held["part"] = held["main"] + held["far"]
        return [held["part"], *held["third"]]

    grad_normed, packed, (upstream, gain_1) = backward_layer(
        w, (cot, above_mine, above_other, x_1, in_gain[1][None], mine, other), wts[0], saved_0, geometry,
        ((), middle, spread),
    )
    far_a = across(packed[0])
    first_half = halves(w, grad_normed)
    got = total_start(w, packed[1], first_half)
    last_got = move(piece(first_half, 1 - w.low, 2), beside)
    part = over_outer(w, sum(got[1:], got[0]))
    last_part = piece(first_half, w.low, 2) + tie(w, last_got, far_a)
    x = piece(x_0, quarter, 4)
    inv_rms = lax.rsqrt(jnp.mean(x * x, axis=1, keepdims=True) + EPSILON)
    scaled = x * inv_rms
    gain_0 = jnp.sum(last_part * scaled, axis=0)
    inner = last_part * in_gain[0]
    last = piece(upstream, quarter, 4) + inv_rms * (
        inner - scaled * jnp.mean(inner * scaled, axis=1, keepdims=True)
    )
    last = tie(w, last, part)
    first_step = hand_step(w, last, last)
    totals = total_end(w, 1, *total_spread(w, tie(w, held["part"], part)), shapes, None)
    third = (tie(w, held["third"][0], last), held["third"][1])
    mixed_out, _ = hand_out_end(w, mixed, [mixed_first, held["second"], third])
    gains = jnp.concatenate([gain_0.reshape(-1, lanes), 0.25 * gain_1[0].reshape(-1, lanes)])
    gains = jnp.pad(gains, ((0, 8 - gains.shape[0]), (0, 0)))
    main_b = part[:shard_rows]
    common = jnp.concatenate([part[shard_rows:], held["start"][shard_rows:], gains])
    common = common + move(common, other_core)
    common = common + move(common, beside)
    rest_b = jnp.concatenate([main_b, common])
    far_b = across(rest_b)
    event = event_of(*first_step, rest_b[shard_rows:])
    second_step = hand_step(w, *(tie(w, array, event) for array in first_step))
    part, got = total_spread(w, jnp.concatenate([packed[0] + far_a, rest_b + far_b]))
    third_step = hand_step(w, *(tie(w, array, event_of(*second_step, far_b)) for array in second_step))
    steps = [first_step, second_step, tuple(tie(w, array, event_of(*got)) for array in third_step)]
    input_grad, crossed = hand_out_end(w, last, steps)
    part = tie(w, part, crossed)
    small = (
        (LAYERS, d, wide), (LAYERS, d), (LAYERS, d, heads), (LAYERS, CONV, lanes), (LAYERS, lanes),
        (LAYERS, CONV, wide), (LAYERS, wide), (LAYERS, heads), (LAYERS, heads), (LAYERS, heads), (LAYERS, lanes),
    )
    (
        grad_gate, grad_value, grad_out, _, state, gain_in, step, taps, off, state_taps, state_off, bias, decay, skip,
        gain_out,
    ) = total_end(w, 0, part, got, shapes, totals, small)
    return (
        mixed_out, input_grad, gain_in, grad_gate, grad_value, state, step, taps, off, state_taps, state_off,
        bias, decay, skip, gain_out, grad_out,
    )


def solution(mesh):
    split = P(None, None, "tensor")
    lane = P(None, "tensor")
    rows = P(("dp", "ctx"), None)
    weights = (P(), split, split, P(), split, split, lane, P(), P(), lane, lane, lane, lane, P(None, "tensor", None))
    return jax.shard_map(
        local,
        mesh=mesh,
        in_specs=(rows, P(("dp", "ctx")), *weights, rows),
        out_specs=(rows, rows, *weights),
        check_vma=False,
    )
```
